32 devices in a mesh: grp: 4 (over x, core), ctx: 8 (over z, y).
Axes of the slice: x: 2, y: 2, z: 4, core: 2. Of those that a mesh axis runs over, the one named last changes fastest.
Arguments:
- inputs: bfloat16 [4, 4096, 2048], P('grp', 'ctx'), may hold values from -6 to 6
- queries: bfloat16 [4, 4096, 1024], P('grp', 'ctx'), may hold values from -6 to 6
- key_heads: bfloat16 [4, 4096, 1024], P('grp', 'ctx'), may hold values from -6 to 6
- value_heads: bfloat16 [4, 4096, 1024], P('grp', 'ctx'), may hold values from -6 to 6
- out_grad: bfloat16 [4, 4096, 1024], P('grp', 'ctx'), may hold values from -6 to 6
- qkv_weight: bfloat16 [2048, 3072], P('ctx'), may hold values from -0.125 to 0.125
- gate_weight: bfloat16 [32, 2048, 768], P(('grp', 'ctx')), may hold values from -0.125 to 0.125
- up_weight: bfloat16 [32, 2048, 768], P(('grp', 'ctx')), may hold values from -0.125 to 0.125
- down_weight: bfloat16 [32, 768, 2048], P(('grp', 'ctx')), may hold values from -0.21875 to 0.21875
- chosen: int32 [4, 8, 32, 2], P('grp', 'ctx'), may hold values from 0 to 511, as said below
- pad_counts: int32 [4, 8, 32], P('grp', 'ctx'), may hold values from 0 to 2, as said below
- combine: float32 [4, 8, 32, 2], P('grp', 'ctx'), may hold values from 0.05 to 1
Outputs:
- input_grad: bfloat16 [4, 4096, 2048], P('grp', 'ctx')
The draws below stay inside these ranges and needn't reach their ends.
Inputs may be any that keep to these rules, and one draw needn't show every extreme that they name: `chosen`: local rows of the listing device; the 2 entries of one list are distinct, and its last pad_counts entries are padding. `pad_counts`: counts of padding entries at the end of the matching list of chosen.
All inputs are finite; a program needn't handle non-finite values.
Results may differ from the reference program's by a relative error of at most 0.015.
Values may be sent and summed in bfloat16 or wider, within the bound.
No kernel may reach another device: no remote copies, remote signals or barrier semaphores. Data moves between devices by JAX's collectives and lax.ppermute only.
A program may use at most 192 MiB of HBM per device.

```python
import math
import jax
import jax.numpy as jnp
from jax import lax

D = 2048
FF = 768
HEADS = 8
DH = 128
BLK = 512
TOK_DEV = 512
SLOT = 2
EXPERTS = 32
LEN = 4096
N_GRP = 4
N_CTX = 8


def routing_tables(key):
    devices = N_GRP * N_CTX
    level_key = jax.random.fold_in(key, 101)
    hot_key = jax.random.fold_in(key, 102)
    cold_key = jax.random.fold_in(key, 103)
    drop_key = jax.random.fold_in(key, 104)
    empty_key = jax.random.fold_in(key, 105)
    score_key = jax.random.fold_in(key, 106)
    expert_ids = jnp.arange(EXPERTS, dtype=jnp.int32)
    source_ids = jnp.arange(devices, dtype=jnp.int32)
    levels = jax.random.randint(level_key, (EXPERTS,), 1, SLOT + 1)
    hottest = jax.random.randint(hot_key, (), 0, EXPERTS)
    coldest = (hottest + 1 + jax.random.randint(cold_key, (), 0, EXPERTS - 1)) % EXPERTS
    levels = jnp.where(expert_ids == hottest, SLOT, levels)
    levels = jnp.where(expert_ids == coldest, 1, levels)
    drops = jax.random.randint(drop_key, (devices, EXPERTS), 0, 2)
    drops = jnp.where(expert_ids[None, :] == hottest, 0, drops)
    empty_source = jax.random.randint(empty_key, (), 0, devices)
    forced = (expert_ids[None, :] == coldest) & (source_ids[:, None] == empty_source)
    drops = jnp.where(forced, 1, drops)
    live = levels[None, :] - drops
    pads = (SLOT - live).astype(jnp.int32)
    scores = jax.random.randint(score_key, (devices, EXPERTS, TOK_DEV), 0, 2 ** 18)
    scores = scores * TOK_DEV + jnp.arange(TOK_DEV, dtype=jnp.int32)
    picked = lax.top_k(scores, SLOT)[1].astype(jnp.int32)
    return (picked.reshape(N_GRP, N_CTX, EXPERTS, SLOT), pads.reshape(N_GRP, N_CTX, EXPERTS))


def draw_chosen(key, part):
    return routing_tables(key)[0]


def draw_pad_counts(key, part):
    return routing_tables(key)[1]


def block_scale(own_key, dims, cuts, low, top_value):
    loudness, own = 1.0, jax.random.fold_in(own_key, 6)
    for axis_at, shards_of in cuts:
        draws = jnp.exp(jax.random.uniform(jax.random.fold_in(own, axis_at), (shards_of,), jnp.float32, low / len(cuts), top_value / len(cuts)))
        loudness = loudness * jnp.repeat(draws, dims[axis_at] // shards_of).reshape([-1 if axis == axis_at else 1 for axis in range(len(dims))])
    return loudness


def noise(stream_key, dims, scale, limit, split=(), kind=jnp.bfloat16):
    drawn = jax.random.normal(stream_key, dims, jnp.float32) * scale
    if len(split) > 0:
        drawn = block_scale(stream_key, dims, split, -0.22, 0.18) * drawn
    return jnp.clip(drawn, min=-limit, max=limit).astype(kind)


def setup_inputs(seed: int = 0) -> dict:
    key_list = jax.random.split(jax.random.key(seed), 13)
    inputs = noise(key_list[0], (N_GRP, LEN, D), 1.0, 6.0, ((0, 4), (1, 8)))
    queries = noise(key_list[1], (N_GRP, LEN, HEADS * DH), 1.0, 6.0, ((0, 4), (1, 8)))
    key_heads = noise(key_list[2], (N_GRP, LEN, HEADS * DH), 1.0, 6.0, ((0, 4), (1, 8)))
    value_heads = noise(key_list[3], (N_GRP, LEN, HEADS * DH), 1.0, 6.0, ((0, 4), (1, 8)))
    out_grad = noise(key_list[4], (N_GRP, LEN, HEADS * DH), 1.0, 6.0, ((0, 4), (1, 8)))
    qkv_weight = noise(key_list[5], (D, 3 * HEADS * DH), D ** -0.5, 0.125, ((0, 8),))
    gate_weight = noise(key_list[6], (EXPERTS, D, FF), D ** -0.5, 0.125, ((0, 32),))
    up_weight = noise(key_list[7], (EXPERTS, D, FF), D ** -0.5, 0.125, ((0, 32),))
    down_weight = noise(key_list[8], (EXPERTS, FF, D), FF ** -0.5, 0.21875, ((0, 32),))
    chosen = draw_chosen(jax.random.fold_in(key_list[12], 71), 0)
    pad_counts = draw_pad_counts(jax.random.fold_in(key_list[12], 71), 0)
    combine = jnp.clip(0.05 + 0.95 * jax.random.uniform(key_list[11], (N_GRP, N_CTX, EXPERTS, SLOT), jnp.float32) ** block_scale(key_list[11], (N_GRP, N_CTX, EXPERTS, SLOT), ((0, 4), (1, 8)), -0.2, 0.2), 0.05, 1.0)
    return {"inputs": inputs, "queries": queries, "key_heads": key_heads, "value_heads": value_heads, "out_grad": out_grad, "qkv_weight": qkv_weight, "gate_weight": gate_weight, "up_weight": up_weight, "down_weight": down_weight, "chosen": chosen, "pad_counts": pad_counts, "combine": combine}


def silu_parts(gate):
    sigma = jax.nn.sigmoid(gate)
    return (gate * sigma, sigma * (1.0 + gate * (1.0 - sigma)))

def expert_front(rows_in, gate_mat, up_mat):
    gate = jnp.dot(rows_in, gate_mat, preferred_element_type=jnp.float32)
    up_proj = jnp.dot(rows_in, up_mat, preferred_element_type=jnp.float32)
    active, slope = silu_parts(gate)
    return (active, up_proj * slope)

def expert_back(rows_grad, weights, active, up_slope, gate_mat, up_mat, down_mat):
    back = jnp.dot(rows_grad, down_mat.T, preferred_element_type=jnp.float32)
    hidden_grad = weights[:, None] * back
    up_grad = (hidden_grad * active).astype(jnp.bfloat16)
    gate_grad = (hidden_grad * up_slope).astype(jnp.bfloat16)
    total = jnp.dot(gate_grad, gate_mat.T, preferred_element_type=jnp.float32)
    total = total + jnp.dot(up_grad, up_mat.T, preferred_element_type=jnp.float32)
    return total.astype(jnp.bfloat16)

def exclusive_sums(states, reverse):
    if reverse:
        states = states[::-1]
    running = jnp.cumsum(states, axis=0)
    shifted = jnp.concatenate([jnp.zeros_like(states[:1]), running[:-1]], axis=0)
    if reverse:
        shifted = shifted[::-1]
    return shifted

def to_half(values):
    rounded = values.astype(jnp.bfloat16)
    rounded = lax.optimization_barrier(rounded)
    return rounded.astype(jnp.float32)

def block_grads(query_blk, key_blk, value_blk, grad_blk, prefix, suffix):
    scaling = 1.0 / math.sqrt(LEN * DH)
    highest = lax.Precision.HIGHEST
    block_rows = query_blk.shape[0]
    causal = lax.broadcasted_iota(jnp.int32, (block_rows, block_rows), 0) >= lax.broadcasted_iota(jnp.int32, (block_rows, block_rows), 1)
    grad_scores = jnp.einsum('thd,shd->hts', grad_blk, value_blk, precision=highest)
    query_scores = jnp.einsum('thd,shd->hts', query_blk, key_blk, precision=highest)
    near_grad = to_half(jnp.where(causal, scaling * grad_scores, 0.0))
    near_query = to_half(jnp.where(causal, scaling * query_scores, 0.0))
    query_grad = jnp.einsum('hts,shd->thd', near_grad, key_blk, precision=highest) + scaling * jnp.einsum('thd,hde->the', grad_blk, prefix, precision=highest)
    key_grad = jnp.einsum('hts,thd->shd', near_grad, query_blk, precision=highest) + scaling * jnp.einsum('shd,hde->she', value_blk, suffix, precision=highest)
    value_grad = jnp.einsum('hts,the->she', near_query, grad_blk, precision=highest) + scaling * jnp.einsum('she,hde->shd', key_blk, suffix, precision=highest)
    return (query_grad.astype(jnp.bfloat16), key_grad.astype(jnp.bfloat16), value_grad.astype(jnp.bfloat16))

def attention_group(queries, key_heads, value_heads, out_grad):
    block_count = LEN // BLK

    def blocks(array):
        return array.reshape(block_count, BLK, HEADS, DH).astype(jnp.float32)
    query_b = blocks(queries)
    key_b = blocks(key_heads)
    value_b = blocks(value_heads)
    grad_b = blocks(out_grad)
    highest = lax.Precision.HIGHEST
    outer_values = jnp.einsum('bthd,bthe->bhde', value_b, key_b, precision=highest)
    outer_grads = jnp.einsum('bthd,bthe->bhde', grad_b, query_b, precision=highest)
    before = exclusive_sums(outer_values, False)
    after = exclusive_sums(outer_grads, True)

    def one_block(packed):
        return block_grads(*packed)
    query_grad, key_grad, value_grad = lax.map(one_block, (query_b, key_b, value_b, grad_b, before, after))
    return jnp.concatenate([query_grad.reshape(LEN, HEADS * DH), key_grad.reshape(LEN, HEADS * DH), value_grad.reshape(LEN, HEADS * DH)], axis=1)

def reference(inputs, queries, key_heads, value_heads, out_grad, qkv_weight, gate_weight, up_weight, down_weight, chosen, pad_counts, combine):

    def group_grad(packed):
        qkv_grad = attention_group(*packed)
        return jnp.dot(qkv_grad, qkv_weight.T, preferred_element_type=jnp.float32).astype(jnp.bfloat16)
    token_grad = lax.map(group_grad, (queries, key_heads, value_heads, out_grad))
    devices = N_GRP * N_CTX
    local_inputs = inputs.reshape(devices, TOK_DEV, D)
    local_grads = token_grad.reshape(devices, TOK_DEV, D)
    chosen_all = chosen.reshape(devices, EXPERTS, SLOT).astype(jnp.int32)
    live = lax.broadcasted_iota(jnp.int32, (devices, EXPERTS, SLOT), 2) < (SLOT - pad_counts.reshape(devices, EXPERTS))[:, :, None]
    slot_weight = jnp.where(live, combine.reshape(devices, EXPERTS, SLOT), 0.0)
    source = lax.broadcasted_iota(jnp.int32, (devices, SLOT), 0)

    def one_expert(packed):
        slot_rows, weights, gate_mat, up_mat, down_mat = packed
        rows_in = local_inputs[source, slot_rows].reshape(devices * SLOT, D)
        rows_grad = local_grads[source, slot_rows].reshape(devices * SLOT, D)
        active, up_slope = expert_front(rows_in, gate_mat, up_mat)
        result = expert_back(rows_grad, weights.reshape(-1), active, up_slope, gate_mat, up_mat, down_mat)
        return result.reshape(devices, SLOT, D)
    per_expert = lax.map(one_expert, (jnp.transpose(chosen_all, (1, 0, 2)), jnp.transpose(slot_weight, (1, 0, 2)), gate_weight, up_weight, down_weight))
    masked = jnp.where(jnp.transpose(live, (1, 0, 2))[:, :, :, None], per_expert.astype(jnp.float32), 0.0)
    source_index = lax.broadcasted_iota(jnp.int32, (EXPERTS, devices, SLOT), 1)
    added = jnp.zeros((devices, TOK_DEV, D), jnp.float32).at[source_index, jnp.transpose(chosen_all, (1, 0, 2))].add(masked)
    total = token_grad.astype(jnp.float32) + added.reshape(N_GRP, LEN, D)
    return total.astype(jnp.bfloat16)
```

```python
import functools
import math

import jax
import jax.numpy as jnp
from jax import lax
from jax.experimental import pallas as pl
from jax.experimental.pallas import tpu as pltpu
from jax.sharding import PartitionSpec as P

DH = 128
VMEM_BYTES = 56 * 1024 * 1024
F32 = jnp.float32
BF16 = jnp.bfloat16
LAST = (((1,), (1,)), ((), ()))
FIRST = (((0,), (0,)), ((), ()))
PLAIN = (((1,), (0,)), ((), ()))


def dot(left, right, contract):
    return lax.dot_general(left, right, contract, preferred_element_type=F32)


def in_vmem():
    return pl.BlockSpec(memory_space=pltpu.VMEM)


def in_smem():
    return pl.BlockSpec(memory_space=pltpu.SMEM)


def anywhere():
    return pl.BlockSpec(memory_space=pl.ANY)


def params():
    return pltpu.CompilerParams(vmem_limit_bytes=VMEM_BYTES)


def cost(flops, moved):
    return pl.CostEstimate(flops=int(flops), bytes_accessed=int(moved), transcendentals=0)


def lane_slice(start, size):
    return pl.ds(pl.multiple_of(start, DH), size)


class Plan:
    def __init__(self):
        self.grp = lax.axis_size("grp")
        self.ctx = lax.axis_size("ctx")
        self.cores = 2 if self.grp % 2 == 0 else 1
        self.cross = self.grp // self.cores
        inner = 1
        while inner * inner * 4 <= self.ctx and self.ctx % (inner * 2) == 0:
            inner *= 2
        self.inner = inner
        self.outer = self.ctx // inner

    def outer_turn(self, k):
        a, b = self.outer, self.inner
        return [(z * b + y, ((z + k) % a) * b + y) for z in range(a) for y in range(b)]

    def inner_turn(self, k):
        a, b = self.outer, self.inner
        return [(z * b + y, z * b + (y + k) % b) for z in range(a) for y in range(b)]

    def cross_turn(self, k):
        m, n = self.cross, self.cores
        return [(x * n + c, ((x + k) % m) * n + c) for x in range(m) for c in range(n)]

    def core_swap(self):
        return [(g, g ^ 1) for g in range(self.grp)]

    def mixed_turn(self, dx, dy):
        pairs = []
        for g in range(self.grp):
            x, c = divmod(g, self.cores)
            for s in range(self.ctx):
                z, y = divmod(s, self.inner)
                if c == 0:
                    to = (((x + dx) % self.cross) * self.cores + c, s)
                else:
                    to = (g, z * self.inner + (y + dy) % self.inner)
                pairs.append((g * self.ctx + s, to[0] * self.ctx + to[1]))
        return pairs


def state_kernel(inner, heads, pos_ref, q_ref, k_ref, v_ref, g_ref, *out_refs):
    each = heads // inner
    for i, out_ref in enumerate(out_refs):
        base = lax.rem(pos_ref[3] + i, inner) * (each * DH)
        for h in range(each):
            lanes = lane_slice(base + h * DH, DH)
            rows = slice(h * DH, (h + 1) * DH)
            out_ref[0, rows, :] = dot(v_ref[:, lanes], k_ref[:, lanes], FIRST).astype(BF16)
            out_ref[1, rows, :] = dot(g_ref[:, lanes], q_ref[:, lanes], FIRST).astype(BF16)


def total_kernel(inner, outer, pos_ref, *refs):
    ins, outs = refs[:inner], refs[inner:]
    total = ins[0][...].astype(F32)
    for ref in ins[1:]:
        total = total + ref[...].astype(F32)
    values, grads = total[0].astype(BF16), total[1].astype(BF16)
    for k, out in enumerate(outs, 1):
        out[...] = jnp.where(pos_ref[2] + k < outer, values, grads)


def spread_kernel(inner, outer, pos_ref, *refs):
    own, far, outs = refs[:inner], refs[inner : inner + outer - 1], refs[inner + outer - 1 :]
    z, y = pos_ref[2], pos_ref[3]
    shape = own[0].shape[1:]
    before = jnp.zeros(shape, F32)
    after = jnp.zeros(shape, F32)
    for k, ref in enumerate(far, 1):
        piece = ref[...].astype(F32)
        before = before + jnp.where(z >= k, piece, 0.0)
        after = after + jnp.where(z < k, piece, 0.0)
    for i, out in enumerate(outs):
        goal = lax.rem(y + i, inner)
        low, high = before, after
        for k, ref in enumerate(own):
            source = lax.rem(y + inner - k, inner)
            low = low + jnp.where(source < goal, ref[0].astype(F32), 0.0)
            high = high + jnp.where(source > goal, ref[1].astype(F32), 0.0)
        out[0] = low.astype(BF16)
        out[1] = high.astype(BF16)


def near_kernel(scaling, q_ref, k_ref, v_ref, g_ref, out_ref):
    rows = q_ref.shape[0]
    q, k, v, g = q_ref[...], k_ref[...], v_ref[...], g_ref[...]
    causal = lax.broadcasted_iota(jnp.int32, (rows, rows), 0) >= lax.broadcasted_iota(
        jnp.int32, (rows, rows), 1
    )
    near_grad = jnp.where(causal, scaling * dot(g, v, LAST), 0.0).astype(BF16)
    near_query = jnp.where(causal, scaling * dot(q, k, LAST), 0.0).astype(BF16)
    out_ref[0] = dot(near_grad, k, PLAIN).astype(BF16)
    out_ref[1] = dot(near_grad, q, FIRST).astype(BF16)
    out_ref[2] = dot(near_query, g, FIRST).astype(BF16)


def pick_matrix(pick_ref, rows):
    count = pick_ref.shape[0]
    return (lax.broadcasted_iota(jnp.int32, (count, rows), 1) == pick_ref[...]).astype(BF16)


def input_rows_kernel(pick_ref, weight_ref, x_ref, out_ref):
    rows, width = x_ref.shape
    out_ref[:, :width] = dot(pick_matrix(pick_ref, rows), x_ref[...], PLAIN).astype(BF16)
    weight = weight_ref[...]
    upper = weight.astype(BF16).astype(F32)
    lane = lax.broadcasted_iota(jnp.int32, (weight.shape[0], DH), 1)
    both = jnp.where(lane == 0, upper, jnp.where(lane == 1, weight - upper, 0.0))
    out_ref[:, width:] = both.astype(BF16)


def far_kernel(inner, heads, scaling, pos_ref, pick_ref, near_ref, k_ref, v_ref, g_ref, *refs):
    states, (qkv_ref, rows_ref) = refs[:inner], refs[inner:]
    each = heads // inner
    rows = k_ref.shape[0]
    for i, state in enumerate(states):
        base = lax.rem(pos_ref[3] + inner - i, inner) * (each * DH)
        for h in range(each):
            lanes = lane_slice(base + h * DH, DH)
            prefix = state[0, h * DH : (h + 1) * DH, :]
            suffix = state[1, h * DH : (h + 1) * DH, :]
            parts = (
                dot(g_ref[:, lanes], prefix, PLAIN),
                dot(v_ref[:, lanes], suffix, PLAIN),
                dot(k_ref[:, lanes], suffix, LAST),
            )
            for n, part in enumerate(parts):
                whole = near_ref[n, :, lanes].astype(F32) + scaling * part
                qkv_ref[:, lane_slice(base + (n * heads + h) * DH, DH)] = whole.astype(BF16)
    rows_ref[...] = dot(pick_matrix(pick_ref, rows), qkv_ref[...], PLAIN).astype(BF16)


def start_pieces(plan, keys, pos_ref, pieces, buffer, sems):
    copies = []
    x = lax.div(pos_ref[0], plan.cores)
    c = lax.rem(pos_ref[0], plan.cores)
    block = buffer.shape[0] // plan.inner
    for n, (key, piece) in enumerate(zip(keys, pieces, strict=True)):
        dx, dc, dy = key
        y = lax.rem(pos_ref[3] + plan.inner - dy, plan.inner)
        start = y * block
        if dx is not None:
            gx = lax.rem(x + plan.cross - dx, plan.cross)
            gc = c if dc == 0 else 1 - c
            start = start + (gx * plan.cores + gc) * piece.shape[0]
        size = piece.shape[0]
        start = pl.multiple_of(start, size)
        copy = pltpu.make_async_copy(piece, buffer.at[pl.ds(start, size), :], sems.at[n])
        copy.start()
        copies.append(copy)
    return copies


def project_kernel(plan, keys, pos_ref, qkv_ref, *refs):
    pieces, (out_ref, buffer, sems) = refs[: len(keys)], refs[len(keys) :]
    for copy in start_pieces(plan, keys, pos_ref, pieces, buffer, sems):
        copy.wait()
    out_ref[...] = dot(qkv_ref[...], buffer[...], LAST).astype(BF16)


def back_kernel(plan, keys, turn, pos_ref, rows_ref, so_far_ref, down_ref, *refs):
    pieces, (out_ref, buffer, down, sems) = refs[: len(keys)], refs[len(keys) :]
    copies = start_pieces(plan, keys, pos_ref, pieces, buffer, sems)
    width = buffer.shape[0]
    z = lax.rem(pos_ref[2] + plan.outer - turn, plan.outer)
    last = pltpu.make_async_copy(
        down_ref.at[:, lane_slice(z * width, width)], down, sems.at[len(keys)]
    )
    last.start()
    for copy in copies:
        copy.wait()
    last.wait()
    grad_rows = dot(rows_ref[...], buffer[...], LAST).astype(BF16)
    out_ref[...] = so_far_ref[...] + dot(grad_rows, down[...], LAST)


def front_kernel(x_ref, gate_ref, up_ref, active_ref, slope_ref, gate_acc, up_acc):
    step = pl.program_id(0)

    @pl.when(step == 0)
    def _():
        gate_acc[...] = jnp.zeros_like(gate_acc)
        up_acc[...] = jnp.zeros_like(up_acc)

    gate_acc[...] += dot(x_ref[...], gate_ref[...], PLAIN)
    up_acc[...] += dot(x_ref[...], up_ref[...], PLAIN)

    @pl.when(step == pl.num_programs(0) - 1)
    def _():
        gate = gate_acc[...]
        sigma = jax.nn.sigmoid(gate)
        active_ref[...] = gate * sigma
        slope_ref[...] = up_acc[...] * (sigma * (1.0 + gate * (1.0 - sigma)))


def slot_kernel(back_ref, weight_ref, active_ref, slope_ref, gate_ref, up_ref, out_ref):
    weight = weight_ref[:, 0:1].astype(F32) + weight_ref[:, 1:2].astype(F32)
    hidden = weight * back_ref[...]
    up_grad = (hidden * active_ref[...]).astype(BF16)
    gate_grad = (hidden * slope_ref[...]).astype(BF16)
    total = dot(gate_grad, gate_ref[...], LAST) + dot(up_grad, up_ref[...], LAST)
    out_ref[...] = total.astype(BF16)


def join_kernel(plan, pos_ref, pick_ref, returned_ref, *refs):
    parts, out_ref = refs[:-1], refs[-1]
    rows, width = parts[0].shape
    spread = pick_matrix(pick_ref, rows)
    for turn, part in enumerate(parts):
        z = lax.rem(pos_ref[2] + plan.outer - turn, plan.outer)
        lanes = lane_slice(z * width, width)
        added = dot(spread, returned_ref[:, lanes], FIRST)
        out_ref[:, lanes] = (part[...].astype(F32) + added).astype(BF16)


def gather_projection(plan, weight):
    share = weight.shape[0] // plan.grp
    core = lax.rem(lax.axis_index("grp"), plan.cores)
    own = lax.dynamic_slice_in_dim(weight, lax.axis_index("grp") * share, share, 0)
    groups = []
    held = own
    for turn in range(plan.outer):
        pieces = {}
        if turn == 0:
            for dy in range(1, plan.inner):
                pieces[0, 0, dy] = lax.ppermute(own, "ctx", plan.inner_turn(dy))
                for dx in range(1, plan.cross):
                    pieces[dx, 0, dy] = lax.ppermute(
                        pieces[0, 0, dy], "grp", plan.cross_turn(dx)
                    )
        else:
            held = lax.ppermute(held, "ctx", plan.outer_turn(1))
            pieces[0, 0, 0] = held
            for dx in range(1, plan.cross):
                pieces[dx, 0, 0] = lax.ppermute(held, "grp", plan.cross_turn(dx))
            for dy in range(1, plan.inner):
                pieces[0, 0, dy] = lax.ppermute(held, "ctx", plan.inner_turn(dy))
            for dx in range(1, plan.cross):
                for dy in range(1, plan.inner):
                    pieces[dx, 0, dy] = lax.ppermute(
                        jnp.where(core == 0, pieces[0, 0, dy], pieces[dx, 0, 0]),
                        ("grp", "ctx"),
                        plan.mixed_turn(dx, dy),
                    )
        if plan.cores == 2:
            for dx, _, dy in list(pieces):
                pieces[dx, 1, dy] = lax.ppermute(pieces[dx, 0, dy], "grp", plan.core_swap())
        if turn == 0:
            pieces[None, None, 0] = weight
        groups.append(pieces)
    return groups


def local(
    inputs,
    queries,
    key_heads,
    value_heads,
    out_grad,
    qkv_weight,
    gate_weight,
    up_weight,
    down_weight,
    chosen,
    pad_counts,
    combine,
):
    plan = Plan()
    rows, width = inputs.shape[1:]
    channels = queries.shape[2]
    heads = channels // DH
    scaling = 1.0 / math.sqrt(plan.ctx * rows * DH)
    q, k, v, g = queries[0], key_heads[0], value_heads[0], out_grad[0]
    gate_mat, up_mat, down_mat = gate_weight[0], up_weight[0], down_weight[0]
    hidden = gate_mat.shape[1]
    experts, slots = chosen.shape[2:]
    items = experts * slots
    inner, outer = plan.inner, plan.outer
    grp_at, ctx_at = lax.axis_index("grp"), lax.axis_index("ctx")
    pos = jnp.stack([grp_at, ctx_at, ctx_at // inner, ctx_at % inner]).astype(jnp.int32)
    live = (
        lax.broadcasted_iota(jnp.int32, (experts, slots), 1)
        < (slots - pad_counts[0, 0])[:, None]
    )
    pick = jnp.where(live, chosen[0, 0], -1).reshape(items, 1)
    slot_weight = jnp.where(live, combine[0, 0], 0.0).reshape(items, 1)

    groups = gather_projection(plan, qkv_weight)

    part = jax.ShapeDtypeStruct((2, channels // inner, DH), BF16)
    own = pl.pallas_call(
        functools.partial(state_kernel, inner, heads),
        out_shape=[part] * inner,
        in_specs=[in_smem()] + [in_vmem()] * 4,
        out_specs=[in_vmem()] * inner,
        compiler_params=params(),
        cost_estimate=cost(4 * rows * DH * channels, 8 * rows * channels),
        name="states",
    )(pos, q, k, v, g)
    shares = [own[0]] + [
        lax.ppermute(own[i], "ctx", plan.inner_turn(i)) for i in range(1, inner)
    ]
    totals = pl.pallas_call(
        functools.partial(total_kernel, inner, outer),
        out_shape=[jax.ShapeDtypeStruct(part.shape[1:], BF16)] * (outer - 1),
        in_specs=[in_smem()] + [in_vmem()] * inner,
        out_specs=[in_vmem()] * (outer - 1),
        compiler_params=params(),
        name="totals",
    )(pos, *shares)
    far = [lax.ppermute(totals[i - 1], "ctx", plan.outer_turn(i)) for i in range(1, outer)]
    sums = pl.pallas_call(
        functools.partial(spread_kernel, inner, outer),
        out_shape=[part] * inner,
        in_specs=[in_smem()] + [in_vmem()] * (inner + outer - 1),
        out_specs=[in_vmem()] * inner,
        compiler_params=params(),
        name="sums",
    )(pos, *shares, *far)
    states = [sums[0]] + [
        lax.ppermute(sums[i], "ctx", plan.inner_turn(i)) for i in range(1, inner)
    ]

    packed = pl.pallas_call(
        input_rows_kernel,
        out_shape=jax.ShapeDtypeStruct((items, width + DH), BF16),
        in_specs=[in_vmem()] * 3,
        out_specs=in_vmem(),
        compiler_params=params(),
        cost_estimate=cost(2 * items * rows * width, 2 * rows * width),
        name="input_rows",
    )(pick, slot_weight, inputs[0])
    head = pl.BlockSpec((rows, DH), lambda h: (0, h))
    near = pl.pallas_call(
        functools.partial(near_kernel, scaling),
        out_shape=jax.ShapeDtypeStruct((3, rows, channels), BF16),
        grid=(heads,),
        in_specs=[head] * 4,
        out_specs=pl.BlockSpec((3, rows, DH), lambda h: (0, 0, h)),
        compiler_params=params(),
        cost_estimate=cost(10 * rows * rows * channels, 14 * rows * channels),
        name="near",
    )(q, k, v, g)

    def exchange(array):
        moved = lax.all_to_all(
            array.reshape(experts, slots, array.shape[1]),
            ("grp", "ctx"),
            split_axis=0,
            concat_axis=0,
            tiled=True,
        )
        return moved.reshape(items, array.shape[1])

    arrived = exchange(packed)
    steps = 4
    deep = pl.BlockSpec((width // steps, hidden), lambda i: (i, 0))
    front_out = jax.ShapeDtypeStruct((items, hidden), F32)
    active, slope = pl.pallas_call(
        front_kernel,
        out_shape=[front_out] * 2,
        grid=(steps,),
        in_specs=[pl.BlockSpec((items, width // steps), lambda i: (0, i)), deep, deep],
        out_specs=[pl.BlockSpec((items, hidden), lambda i: (0, 0))] * 2,
        scratch_shapes=[pltpu.VMEM((items, hidden), F32)] * 2,
        compiler_params=params(),
        cost_estimate=cost(4 * items * width * hidden, 4 * width * hidden),
        name="front",
    )(arrived[:, :width], gate_mat, up_mat)

    qkv_grad, sent_rows = pl.pallas_call(
        functools.partial(far_kernel, inner, heads, scaling),
        out_shape=[
            jax.ShapeDtypeStruct((rows, 3 * channels), BF16),
            jax.ShapeDtypeStruct((items, 3 * channels), BF16),
        ],
        in_specs=[in_smem()] + [in_vmem()] * (5 + inner),
        out_specs=[in_vmem()] * 2,
        compiler_params=params(),
        cost_estimate=cost(6 * rows * DH * channels, 18 * rows * channels),
        name="far",
    )(pos, pick, near, k, v, g, *states)
    grad_rows = exchange(sent_rows)

    span = inner * qkv_weight.shape[0]
    buffer = pltpu.VMEM((span, 3 * channels), BF16)
    token_parts = []
    back = jnp.zeros((items, hidden), F32)
    for turn, group in enumerate(groups):
        keys, pieces = list(group), list(group.values())
        back = pl.pallas_call(
            functools.partial(back_kernel, plan, keys, turn),
            out_shape=jax.ShapeDtypeStruct((items, hidden), F32),
            in_specs=[in_smem(), in_vmem(), in_vmem(), anywhere()] + [anywhere()] * len(keys),
            out_specs=in_vmem(),
            scratch_shapes=[
                buffer,
                pltpu.VMEM((hidden, span), BF16),
                pltpu.SemaphoreType.DMA((len(keys) + 1,)),
            ],
            compiler_params=params(),
            cost_estimate=cost(2 * items * span * (3 * channels + hidden), 6 * span * channels),
            name="back",
        )(pos, grad_rows, back, down_mat, *pieces)
        token_parts.append(
            pl.pallas_call(
                functools.partial(project_kernel, plan, keys),
                out_shape=jax.ShapeDtypeStruct((rows, span), BF16),
                in_specs=[in_smem(), in_vmem()] + [anywhere()] * len(keys),
                out_specs=in_vmem(),
                scratch_shapes=[buffer, pltpu.SemaphoreType.DMA((len(keys),))],
                compiler_params=params(),
                cost_estimate=cost(6 * rows * span * channels, 6 * (span + rows) * channels),
                name="project",
            )(pos, qkv_grad, *pieces)
        )
    wide = pl.BlockSpec((width // steps, hidden), lambda i: (i, 0))
    fixed = pl.BlockSpec((items, hidden), lambda i: (0, 0))
    slot_grad = pl.pallas_call(
        slot_kernel,
        out_shape=jax.ShapeDtypeStruct((items, width), BF16),
        grid=(steps,),
        in_specs=[fixed, pl.BlockSpec((items, DH), lambda i: (0, width // DH)), fixed, fixed]
        + [wide, wide],
        out_specs=pl.BlockSpec((items, width // steps), lambda i: (0, i)),
        compiler_params=params(),
        cost_estimate=cost(4 * items * width * hidden, 4 * width * hidden),
        name="slot",
    )(back, arrived, active, slope, gate_mat, up_mat)
    returned = exchange(slot_grad)
    total = pl.pallas_call(
        functools.partial(join_kernel, plan),
        out_shape=jax.ShapeDtypeStruct((rows, width), BF16),
        in_specs=[in_smem()] + [in_vmem()] * (2 + outer),
        out_specs=in_vmem(),
        compiler_params=params(),
        cost_estimate=cost(2 * items * rows * width, 4 * rows * width),
        name="join",
    )(pos, pick, returned, *token_parts)
    return total[None]


def solution(mesh):
    rows = P("grp", "ctx", None)
    expert = P(("grp", "ctx"), None, None)
    lists = P("grp", "ctx", None, None)
    return jax.shard_map(
        local,
        mesh=mesh,
        in_specs=(rows,) * 5 + (P("ctx", None),) + (expert,) * 3 + (lists, rows, lists),
        out_specs=rows,
        check_vma=False,
    )
```

```python
import functools
import math

import jax
import jax.numpy as jnp
from jax import lax
from jax.experimental import pallas as pl
from jax.experimental.pallas import tpu as pltpu
from jax.sharding import PartitionSpec as P

DH = 128
MIB = 1024 * 1024
LARGE = 52
F32 = jnp.float32
BF16 = jnp.bfloat16
LAST = (((1,), (1,)), ((), ()))
FIRST = (((0,), (0,)), ((), ()))
PLAIN = (((1,), (0,)), ((), ()))


def dot(left, right, contract):
    return lax.dot_general(left, right, contract, preferred_element_type=F32)


def in_vmem():
    return pl.BlockSpec(memory_space=pltpu.VMEM)


def in_smem():
    return pl.BlockSpec(memory_space=pltpu.SMEM)


def anywhere():
    return pl.BlockSpec(memory_space=pl.ANY)


def params(mib=6):
    return pltpu.CompilerParams(vmem_limit_bytes=mib * MIB)


def small():
    return pl.CostEstimate(flops=1, bytes_accessed=1, transcendentals=0)


def lane_slice(start, size):
    return pl.ds(pl.multiple_of(start, DH), size)


class Plan:
    def __init__(self):
        self.grp = lax.axis_size("grp")
        self.ctx = lax.axis_size("ctx")
        self.cores = 2 if self.grp % 2 == 0 else 1
        self.cross = self.grp // self.cores
        inner = 1
        while inner * inner * 4 <= self.ctx and self.ctx % (inner * 2) == 0:
            inner *= 2
        self.inner = inner
        self.outer = self.ctx // inner

    def outer_turn(self, k):
        a, b = self.outer, self.inner
        return [(z * b + y, ((z + k) % a) * b + y) for z in range(a) for y in range(b)]

    def inner_turn(self, k):
        a, b = self.outer, self.inner
        return [(z * b + y, z * b + (y + k) % b) for z in range(a) for y in range(b)]

    def pairs(self, go):
        found = []
        for g in range(self.grp):
            x, c = divmod(g, self.cores)
            for at in range(self.ctx):
                z, y = divmod(at, self.inner)
                goal = go(x, c, z, y)
                if goal is not None:
                    x2, c2, z2, y2 = goal
                    to = (x2 % self.cross * self.cores + c2) * self.ctx
                    found.append((g * self.ctx + at, to + z2 * self.inner + y2 % self.inner))
        return found

    def move(self, array, go):
        return lax.ppermute(array, ("grp", "ctx"), self.pairs(go))

    def swap(self, array):
        return self.move(array, lambda x, c, z, y: (x, 1 - c, z, y))


def state_kernel(inner, turn, pos_ref, q_ref, k_ref, v_ref, g_ref, out_ref):
    each = out_ref.shape[1]
    base = lax.rem(pos_ref[3] + turn, inner) * each
    for h in range(each // DH):
        lanes = lane_slice(base + h * DH, DH)
        rows = slice(h * DH, (h + 1) * DH)
        out_ref[0, rows, :] = dot(v_ref[:, lanes], k_ref[:, lanes], FIRST).astype(BF16)
        out_ref[1, rows, :] = dot(g_ref[:, lanes], q_ref[:, lanes], FIRST).astype(BF16)


def total_kernel(inner, outer, pos_ref, *refs):
    ins, outs = refs[:inner], refs[inner:]
    total = ins[0][...].astype(F32)
    for ref in ins[1:]:
        total = total + ref[...].astype(F32)
    values, grads = total[0].astype(BF16), total[1].astype(BF16)
    for k, out in enumerate(outs, 1):
        out[...] = jnp.where(pos_ref[2] + k < outer, values, grads)


def spread_kernel(inner, outer, pos_ref, *refs):
    own, far, outs = refs[:inner], refs[inner : inner + outer - 1], refs[inner + outer - 1 :]
    z, y = pos_ref[2], pos_ref[3]
    shape = own[0].shape[1:]
    before = jnp.zeros(shape, F32)
    after = jnp.zeros(shape, F32)
    for k, ref in enumerate(far, 1):
        piece = ref[...].astype(F32)
        before = before + jnp.where(z >= k, piece, 0.0)
        after = after + jnp.where(z < k, piece, 0.0)
    for i, out in enumerate(outs):
        goal = lax.rem(y + i, inner)
        low, high = before, after
        for k, ref in enumerate(own):
            source = lax.rem(y + inner - k, inner)
            low = low + jnp.where(source < goal, ref[0].astype(F32), 0.0)
            high = high + jnp.where(source > goal, ref[1].astype(F32), 0.0)
        out[0] = low.astype(BF16)
        out[1] = high.astype(BF16)


def near_kernel(scaling, first, pos_ref, q_ref, k_ref, v_ref, g_ref, out_ref):
    rows = q_ref.shape[0]
    half = rows // 2
    early, late = slice(0, half), slice(half, rows)
    row = lax.broadcasted_iota(jnp.int32, (half, half), 0)
    column = lax.broadcasted_iota(jnp.int32, (half, half), 1)

    def scores(left, right, keep):
        value = scaling * dot(left, right, LAST)
        if keep is not None:
            value = jnp.where(keep, value, 0.0)
        return value.astype(BF16)

    def past(left, right, values):
        first = scores(left[early], right[early], row >= column)
        cross = scores(left[late], right[early], None)
        second = scores(left[late], right[late], row >= column)
        low = dot(first, values[early], PLAIN)
        high = dot(cross, values[early], PLAIN) + dot(second, values[late], PLAIN)
        return low, high

    def future(left, right, values):
        first = scores(left[early], right[early], row <= column)
        cross = scores(left[early], right[late], None)
        second = scores(left[late], right[late], row <= column)
        low = dot(first, values[early], PLAIN) + dot(cross, values[late], PLAIN)
        high = dot(second, values[late], PLAIN)
        return low, high

    def one_head(h, carry):
        lanes = lane_slice((first + h) * DH, DH)
        q, k, v, g = q_ref[:, lanes], k_ref[:, lanes], v_ref[:, lanes], g_ref[:, lanes]
        goal = lane_slice(h * DH, DH)
        for n, (low, high) in enumerate((past(g, v, k), future(v, g, q), future(k, q, g))):
            out_ref[n, early, goal] = low.astype(BF16)
            out_ref[n, late, goal] = high.astype(BF16)
        return carry

    lax.fori_loop(0, out_ref.shape[2] // DH, one_head, 0)


def input_rows_kernel(chosen_ref, pad_ref, combine_ref, x_ref, out_ref, picks_ref, ones, tail):
    rows, width = x_ref.shape
    slots = chosen_ref.shape[3]
    row = lax.broadcasted_iota(jnp.int32, (1, rows), 1)
    lane = lax.broadcasted_iota(jnp.int32, (1, DH), 1)

    def one_slot(n, carry):
        expert, slot = lax.div(n, slots), lax.rem(n, slots)
        live = slot < slots - pad_ref[0, 0, expert]
        token = jnp.where(live, chosen_ref[0, 0, expert, slot], -1)
        ones[pl.ds(n, 1), :] = jnp.where(row == token, 1.0, 0.0)
        weight = jnp.full((1, DH), jnp.where(live, combine_ref[0, 0, expert, slot], 0.0), F32)
        upper = weight.astype(BF16).astype(F32)
        both = jnp.where(lane == 0, upper, jnp.where(lane == 1, weight - upper, 0.0))
        tail[pl.ds(n, 1), :] = both
        return carry

    lax.fori_loop(0, out_ref.shape[0], one_slot, 0)
    picks = ones[...].astype(BF16)
    picks_ref[...] = picks
    out_ref[:, :width] = dot(picks, x_ref[...], PLAIN).astype(BF16)
    out_ref[:, width:] = tail[...].astype(BF16)


def far_kernel(plan, cuts, scaling, pos_ref, picks_ref, k_ref, v_ref, g_ref, *refs):
    inner = plan.inner
    states, near, (qkv_ref, rows_ref) = refs[:inner], refs[inner : inner + cuts], refs[-2:]
    picks = picks_ref[...]
    x = lax.div(pos_ref[0], plan.cores)
    depth = qkv_ref.shape[1] // plan.cross
    rows, channels = k_ref.shape
    heads = channels // DH
    each = heads // inner
    for h in range(heads):
        lanes = slice(h * DH, (h + 1) * DH)
        turn = lax.rem(pos_ref[3] + inner - h // each, inner)
        inside = slice((h % each) * DH, (h % each + 1) * DH)
        pair = states[0][:, inside, :]
        for i in range(1, inner):
            pair = jnp.where(turn == i, states[i][:, inside, :], pair)
        parts = (
            dot(g_ref[:, lanes], pair[0], PLAIN),
            dot(v_ref[:, lanes], pair[1], PLAIN),
            dot(k_ref[:, lanes], pair[1], LAST),
        )
        share = heads // cuts
        near_lanes = slice((h % share) * DH, (h % share + 1) * DH)
        for n, part in enumerate(parts):
            whole = near[h // share][n, :, near_lanes].astype(F32) + scaling * part
            whole = whole.astype(BF16)
            part_at, inside_at = divmod((n * heads + h) * DH, depth)
            start = lax.rem(x + plan.cross - part_at, plan.cross) * depth + inside_at
            qkv_ref[:, lane_slice(start, DH)] = whole
            start = (n * heads + h) * DH
            rows_ref[:, start : start + DH] = dot(picks, whole, PLAIN).astype(BF16)


def turn_kernel(pos_ref, in_ref, out_ref):
    out_ref[...] = in_ref[...].T


def turned(plan, weight, pos, mode):
    block = (weight.shape[0], weight.shape[1] // plan.grp)
    cross, cores = plan.cross, plan.cores
    steps = {"own": 1, "part": cores, "whole": plan.grp}[mode]

    def source(n, at):
        if mode == "whole":
            return (0, n)
        return (0, at[0] // cores * cores + n if mode == "part" else at[0])

    def place(n, at):
        if mode != "whole":
            return (n, 0)
        return (lax.rem(at[0] // cores + cross - n // cores, cross) * cores + n % cores, 0)

    return pl.pallas_call(
        turn_kernel,
        out_shape=jax.ShapeDtypeStruct((steps * block[1], weight.shape[0]), BF16),
        grid_spec=pltpu.PrefetchScalarGridSpec(
            num_scalar_prefetch=1,
            grid=(steps,),
            in_specs=[pl.BlockSpec(block, source)],
            out_specs=pl.BlockSpec((block[1], block[0]), place),
        ),
        compiler_params=params(),
        cost_estimate=small(),
        name="turned",
    )(pos, weight)


class Pieces:
    def __init__(self, plan, entries, pos_ref, refs, ring, sems):
        self.plan, self.pos_ref, self.ring, self.sems = plan, pos_ref, ring, sems
        self.core = lax.rem(pos_ref[0], plan.cores)
        self.found = {}
        sources = list(refs)
        for turn, dx, dy, skip, first in entries:
            pair = [sources.pop(0) for _ in range(1 if first is None else 2)]
            self.found.setdefault((turn, dy), []).append((dx, skip, first, pair))
        for n in range(len(self.found)):
            self.copy(n, True)

    def copy(self, n, start):
        depth = self.ring.shape[1] // self.plan.cross
        parts = list(self.found.values())[n]
        for m, (dx, skip, first, pair) in enumerate(parts):
            deep = pair[0].shape[0]
            at = 0 if dx is None else dx * depth + skip * (depth // 2)
            goal = self.ring.at[n, pl.ds(at, deep), :]
            copy = pltpu.make_async_copy(pair[0], goal, self.sems.at[n, m])
            if not start:
                copy.wait()
            elif first is None:
                copy.start()
            else:
                other = pltpu.make_async_copy(pair[1], goal, self.sems.at[n, m])
                pl.when(self.core == first)(copy.start)
                pl.when(self.core != first)(other.start)

    def blocks(self):
        plan = self.plan
        wide = self.ring.shape[2]
        for n, (turn, dy) in enumerate(self.found):
            self.copy(n, False)
            z = lax.rem(self.pos_ref[2] + plan.outer - turn, plan.outer)
            y = lax.rem(self.pos_ref[3] + plan.inner - dy, plan.inner)
            yield lane_slice((z * plan.inner + y) * wide, wide), self.ring.at[n]


def ring_scratch(found):
    wide = found[0][1][0].shape[1]
    depths = {}
    for (turn, _, dy, _, _), buffers in found:
        depths[turn, dy] = depths.get((turn, dy), 0) + buffers[0].shape[0]
    ring = pltpu.VMEM((len(depths), max(depths.values()), wide), BF16)
    return [ring, pltpu.SemaphoreType.DMA((len(depths), len(found)))]


def reach_blocks(plan, pos_ref, rows_ref, pieces, turned_ref):
    x = lax.div(pos_ref[0], plan.cores)
    depth = turned_ref.shape[1] // plan.cross
    for dx in range(plan.cross):
        lanes = lane_slice(lax.rem(x + plan.cross - dx, plan.cross) * depth, depth)
        turned_ref[:, dx * depth : (dx + 1) * depth] = rows_ref[:, lanes]
    return [
        (lanes, dot(turned_ref[...], block[...], PLAIN).astype(BF16))
        for lanes, block in pieces.blocks()
    ]


def start_loads(sems, *pairs):
    loads = [pltpu.make_async_copy(x, y, sems.at[n]) for n, (x, y) in enumerate(pairs)]
    for load in loads:
        load.start()
    return loads


def reach_kernel(plan, entries, pos_ref, rows_ref, down_hbm, *refs):
    pieces, (back_ref, turned_ref, down_ref, loaded, ring, sems) = refs[:-6], refs[-6:]
    pieces = Pieces(plan, entries, pos_ref, pieces, ring, sems)
    (load,) = start_loads(loaded, (down_hbm, down_ref))
    blocks = reach_blocks(plan, pos_ref, rows_ref, pieces, turned_ref)
    load.wait()
    back_ref[...] = jnp.zeros_like(back_ref)
    for lanes, grads in blocks:
        back_ref[...] += dot(down_ref[:, lanes], grads, LAST)


def expert_kernel(plan, entries, pos_ref, rows_ref, packed_ref, back_ref, *refs):
    hbm, refs = refs[:3], refs[3:]
    pieces, (out_ref, held, turned_ref) = refs[:-9], refs[-9:-6]
    (gate_ref, up_ref, down_ref), (loaded, ring, sems) = refs[-6:-3], refs[-3:]
    pieces = Pieces(plan, entries, pos_ref, pieces, ring, sems)
    loads = start_loads(loaded, *zip(hbm, (gate_ref, up_ref, down_ref), strict=True))
    blocks = reach_blocks(plan, pos_ref, rows_ref, pieces, turned_ref)
    width = out_ref.shape[1]
    loads[0].wait()
    gate = dot(packed_ref[:, :width], gate_ref[...], PLAIN)
    loads[1].wait()
    up = dot(packed_ref[:, :width], up_ref[...], PLAIN)
    sigma = jax.nn.sigmoid(gate)
    active = gate * sigma
    slope = up * (sigma * (1.0 + gate * (1.0 - sigma)))
    loads[2].wait()
    held[...] = back_ref[...]
    for lanes, grads in blocks:
        held[...] += dot(down_ref[:, lanes], grads, LAST)
    weight = packed_ref[:, width : width + 1].astype(F32)
    weight = weight + packed_ref[:, width + 1 : width + 2].astype(F32)
    hidden = weight * held[...].T
    up_grad = (hidden * active).astype(BF16)
    gate_grad = (hidden * slope).astype(BF16)
    steps = 4
    for n in range(steps):
        some = slice(n * width // steps, (n + 1) * width // steps)
        total = dot(gate_ref[some], gate_grad, LAST) + dot(up_ref[some], up_grad, LAST)
        out_ref[:, some] = total.T.astype(BF16)


def project_kernel(plan, entries, pos_ref, qkv_hbm, *refs):
    pieces, (out_ref, qkv_ref, loaded, ring, sems) = refs[:-5], refs[-5:]
    (load,) = start_loads(loaded, (qkv_hbm, qkv_ref))
    pieces = Pieces(plan, entries, pos_ref, pieces, ring, sems)
    load.wait()
    half = out_ref.shape[0] // 2
    depth = qkv_ref.shape[1] // plan.cross
    for lanes, block in pieces.blocks():
        for n in range(2):
            rows = slice(n * half, (n + 1) * half)
            total = None
            for dx in range(plan.cross):
                deep = slice(dx * depth, (dx + 1) * depth)
                term = dot(qkv_ref[rows, deep], block[deep, :], PLAIN)
                total = term if total is None else total + term
            out_ref[rows, lanes] = total.astype(BF16)


def join_kernel(picks_ref, returned_ref, token_ref, out_ref):
    added = dot(picks_ref[...], returned_ref[...], FIRST)
    out_ref[...] = (token_ref[...].astype(F32) + added).astype(BF16)


def together(*values):
    return lax.optimization_barrier(values)


class Turn:
    def __init__(self, plan, turn, held):
        self.plan, self.turn, self.held = plan, turn, held
        self.core = lax.rem(lax.axis_index("grp"), plan.cores)
        self.first = self.mixed(held)

    def mixed(self, array):
        plan, moved = self.plan, {}
        for k in range(1, max(plan.cross, plan.inner)):

            def go(x, c, z, y, k=k):
                if c == 0:
                    return (x + k, c, z, y) if k < plan.cross else None
                return (x, c, z, y + k) if k < plan.inner else None

            moved[k] = plan.move(array, go)
        return moved

    def swap(self):
        self.other = self.plan.swap(self.held)

    def again(self):
        self.second = self.mixed(self.other)

    def turn_corners(self):
        plan = self.plan
        self.corners = {}
        for dx in range(1, plan.cross):
            for dy in range(1, plan.inner):
                sent = self.second[dx]
                if dx != dy:
                    sent = jnp.where(self.core == 0, sent, self.second[dy])

                def go(x, c, z, y, dx=dx, dy=dy):
                    return (x, c, z, y + dy) if c == 0 else (x + dx, c, z, y)

                self.corners[dx, dy] = plan.move(sent, go)

    def pieces(self):
        plan, turn = self.plan, self.turn
        found = [((turn, 0, 0, n, n), (self.held, self.other)) for n in range(2)]
        for k, array in self.first.items():
            first = (array, plan.swap(array))
            second = (self.second[k], plan.swap(self.second[k]))
            if k < plan.cross:
                found.append(((turn, k, 0, 0, 0), first))
                found.append(((turn, k, 0, 1, 0), second))
            if k < plan.inner:
                found.append(((turn, 0, k, 0, 1), second))
                found.append(((turn, 0, k, 1, 1), first))
        for (dx, dy), array in self.corners.items():
            pair = (array, plan.swap(array))
            found.append(((turn, dx, dy, 0, 1), pair))
            found.append(((turn, dx, dy, 1, 0), pair))
        return found


def local(
    inputs,
    queries,
    key_heads,
    value_heads,
    out_grad,
    qkv_weight,
    gate_weight,
    up_weight,
    down_weight,
    chosen,
    pad_counts,
    combine,
):
    plan = Plan()
    rows, width = inputs.shape[1:]
    channels = queries.shape[2]
    heads = channels // DH
    scaling = 1.0 / math.sqrt(plan.ctx * rows * DH)
    q, k, v, g = queries[0], key_heads[0], value_heads[0], out_grad[0]
    gate_mat, up_mat, down_mat = gate_weight[0], up_weight[0], down_weight[0]
    hidden = gate_mat.shape[1]
    experts, slots = chosen.shape[2:]
    items = experts * slots
    inner, outer = plan.inner, plan.outer
    grp_at, ctx_at = lax.axis_index("grp"), lax.axis_index("ctx")
    pos = jnp.stack([grp_at, ctx_at, ctx_at // inner, ctx_at % inner]).astype(jnp.int32)
    across = range(1, plan.cross)
    part = jax.ShapeDtypeStruct((2, channels // inner, DH), BF16)
    own = [None] * inner
    for i in reversed(range(inner)):
        own[i] = pl.pallas_call(
            functools.partial(state_kernel, inner, i),
            out_shape=part,
            in_specs=[in_smem()] + [in_vmem()] * 4,
            out_specs=in_vmem(),
            compiler_params=params(),
            cost_estimate=small(),
            name="states",
        )(pos, q, k, v, g)
    shares = [lax.ppermute(own[i], "ctx", plan.inner_turn(i)) for i in range(1, inner)]
    (later, *_) = together(pos, own[-1])
    held = turned(plan, qkv_weight, later, "own")
    held = lax.ppermute(held, "ctx", plan.outer_turn(1))
    packed, picks = pl.pallas_call(
        input_rows_kernel,
        out_shape=[
            jax.ShapeDtypeStruct((items, width + DH), BF16),
            jax.ShapeDtypeStruct((items, rows), BF16),
        ],
        in_specs=[in_smem()] * 3 + [in_vmem()],
        out_specs=[in_vmem()] * 2,
        scratch_shapes=[pltpu.VMEM((items, rows), F32), pltpu.VMEM((items, DH), F32)],
        compiler_params=params(),
        cost_estimate=small(),
        name="input_rows",
    )(chosen, pad_counts, combine, inputs[0])
    packed, picks, *shares = together(packed, picks, own[0], *shares)
    totals = pl.pallas_call(
        functools.partial(total_kernel, inner, outer),
        out_shape=[jax.ShapeDtypeStruct(part.shape[1:], BF16)] * (outer - 1),
        in_specs=[in_smem()] + [in_vmem()] * inner,
        out_specs=[in_vmem()] * (outer - 1),
        compiler_params=params(),
        cost_estimate=small(),
        name="totals",
    )(pos, *shares)
    after_totals, *totals = together(pos, *totals)
    far = [lax.ppermute(totals[i - 1], "ctx", plan.outer_turn(i)) for i in range(1, outer)]
    aside = turned(plan, qkv_weight, after_totals, "part")
    beside = [
        plan.move(aside, lambda x, c, z, y, dy=dy: (x, c, z, y + dy) if c == 1 else None)
        for dy in range(1, inner)
    ]

    cuts = 2 if heads % 2 == 0 else 1

    def near_part(cut, after):
        return pl.pallas_call(
            functools.partial(near_kernel, scaling, cut * (heads // cuts)),
            out_shape=jax.ShapeDtypeStruct((3, rows, channels // cuts), BF16),
            in_specs=[in_smem()] + [in_vmem()] * 4,
            out_specs=in_vmem(),
            compiler_params=params(),
            cost_estimate=small(),
            name="near",
        )(after, q, k, v, g)

    near = [near_part(0, after_totals)]
    after_near, held, near[0], *arrived = together(after_totals, held, near[0], *far[:1])
    far[:1] = arrived
    turns = []
    if outer > 1:
        turns.append(Turn(plan, 1, held))
        turns[0].swap()
    if outer > 2:
        held = lax.ppermute(held, "ctx", plan.outer_turn(1))
    near += [near_part(cut, after_near) for cut in range(1, cuts)]
    if turns:
        near[-1], turns[0].other = together(near[-1], turns[0].other)
        turns[0].again()

    def exchange(array):
        return lax.all_to_all(array, ("grp", "ctx"), split_axis=0, concat_axis=0, tiled=True)

    shares[0], *arrived = together(shares[0], *far, *near, *beside)
    far, near = arrived[: outer - 1], arrived[outer - 1 : outer - 1 + cuts]
    beside = arrived[outer - 1 + cuts :]
    sums = pl.pallas_call(
        functools.partial(spread_kernel, inner, outer),
        out_shape=[part] * inner,
        in_specs=[in_smem()] + [in_vmem()] * (inner + outer - 1),
        out_specs=[in_vmem()] * inner,
        compiler_params=params(),
        cost_estimate=small(),
        name="sums",
    )(pos, *shares, *far)
    states = [lax.ppermute(sums[i], "ctx", plan.inner_turn(i)) for i in range(1, inner)]
    state = sums[0]
    behind = []
    if turns:
        state, held, *arrived = together(state, held, *turns[0].first.values())
        turns[0].first = dict(zip(turns[0].first, arrived, strict=True))
    moving = dict(turns[0].second) if turns else {}
    if outer > 2:
        turns.append(Turn(plan, 2, held))
        turns[1].swap()
        if outer > 3:
            held = lax.ppermute(held, "ctx", plan.outer_turn(1))
        behind = [held, turns[1].other, *turns[1].first.values()]
    state, *arrived = together(state, *states, *moving.values(), *behind)
    states, arrived = [state, *arrived[: len(states)]], arrived[len(states) :]
    if turns:
        turns[0].second = dict(zip(moving, arrived, strict=False))
        turns[0].turn_corners()
        arrived = arrived[len(moving) :]
    if outer > 2:
        held, turns[1].other, *arrived = arrived
        turns[1].first = dict(zip(turns[1].first, arrived, strict=True))
        turns[1].again()

    qkv_grad, sent_rows = pl.pallas_call(
        functools.partial(far_kernel, plan, cuts, scaling),
        out_shape=[
            jax.ShapeDtypeStruct((rows, 3 * channels), BF16),
            jax.ShapeDtypeStruct((items, 3 * channels), BF16),
        ],
        in_specs=[in_smem()] + [in_vmem()] * (4 + inner + cuts),
        out_specs=[in_vmem()] * 2,
        compiler_params=params(8),
        cost_estimate=small(),
        name="far",
    )(pos, picks, k, v, g, *states, *near)
    for turn in range(3, outer):
        if turn > 3:
            held = lax.ppermute(held, "ctx", plan.outer_turn(1))
        turns.append(Turn(plan, turn, held))
        turns[-1].swap()
    qkv_grad, *beside = together(qkv_grad, *beside)
    aside = [
        [plan.move(x0, lambda x, c, z, y, dx=dx: (x + dx, c, z, y) if c == 1 else None) for dx in across]
        for x0 in beside
    ]
    others = [turn.other for turn in turns[2:]]
    for turn in turns[2:]:
        turn.again()
    sent_rows, *_ = together(sent_rows, *others)
    grad_rows = exchange(sent_rows)
    waits = [turn.first for turn in turns] + [turns[0].corners] + [turn.second for turn in turns[:2]]
    waits.append(dict(enumerate(beside)))
    waits += [dict(enumerate(arrays)) for arrays in aside]
    flat = [array for wait in waits for array in wait.values()]
    grad_rows, packed, *arrived = together(grad_rows, packed, *flat)
    came = exchange(packed)
    for wait in waits:
        for key in wait:
            wait[key] = arrived.pop(0)
    beside, aside = waits[-1 - len(aside)], waits[len(waits) - len(aside) :]
    if outer > 2:
        turns[1].turn_corners()
    whole = turned(plan, qkv_weight, later, "whole")
    found = [((0, None, 0, 0, None), (whole,))]
    for turn in turns[:-1]:
        found.extend(turn.pieces())
    for dy in range(1, inner):
        for dx in range(plan.cross):
            array = beside[dy - 1] if dx == 0 else aside[dy - 1][dx - 1]
            copied = plan.move(array, lambda x, c, z, y: (x, 0, z, y) if c == 1 else None)
            found.append(((0, dx, dy, 0, 1), (array, copied)))

    def some(keep):
        kept = [item for item in found if keep(item[0][0])]
        return kept, [item[0] for item in kept], [x for item in kept for x in item[1]]

    span = inner * qkv_weight.shape[0]

    turned_rows = pltpu.VMEM((items, 3 * channels), BF16)
    qkv_held = pltpu.VMEM((rows, 3 * channels), BF16)
    down_held = pltpu.VMEM((hidden, width), BF16)

    split = max(outer - 2, 1)
    kept, entries, pieces = some(lambda turn: turn < split)
    back = pl.pallas_call(
        functools.partial(reach_kernel, plan, entries),
        out_shape=jax.ShapeDtypeStruct((hidden, items), F32),
        in_specs=[in_smem(), in_vmem()] + [anywhere()] * (1 + len(pieces)),
        out_specs=in_vmem(),
        scratch_shapes=[
            *(turned_rows, down_held, pltpu.SemaphoreType.DMA((1,))),
            *ring_scratch(kept),
        ],
        compiler_params=params(LARGE),
        cost_estimate=small(),
        name="reach",
    )(pos, grad_rows, down_mat, *pieces)
    if turns:
        last = turns[-1]
        if outer > 2:
            last.turn_corners()
        back, *arrived = together(back, *last.corners.values())
        last.corners = dict(zip(last.corners, arrived, strict=True))
    if turns:
        found.extend(turns[-1].pieces())
    kept, entries, pieces = some(lambda turn: turn >= split)
    slot_grad = pl.pallas_call(
        functools.partial(expert_kernel, plan, entries),
        out_shape=jax.ShapeDtypeStruct((items, width), BF16),
        in_specs=[in_smem()] + [in_vmem()] * 3 + [anywhere()] * (3 + len(pieces)),
        out_specs=in_vmem(),
        scratch_shapes=[
            *(pltpu.VMEM((hidden, items), F32), turned_rows),
            *[pltpu.VMEM((width, hidden), BF16)] * 2,
            *(down_held, pltpu.SemaphoreType.DMA((3,))),
            *ring_scratch(kept),
        ],
        compiler_params=params(LARGE),
        cost_estimate=small(),
        name="expert",
    )(pos, grad_rows, came, back, gate_mat, up_mat, down_mat, *pieces)
    returned = exchange(slot_grad)
    kept, entries, pieces = some(lambda turn: True)
    (after_expert, *_) = together(pos, slot_grad)
    token_grad = pl.pallas_call(
        functools.partial(project_kernel, plan, entries),
        out_shape=jax.ShapeDtypeStruct((rows, width), BF16),
        in_specs=[in_smem()] + [anywhere()] * (1 + len(pieces)),
        out_specs=in_vmem(),
        scratch_shapes=[qkv_held, pltpu.SemaphoreType.DMA((1,)), *ring_scratch(kept)],
        compiler_params=params(LARGE),
        cost_estimate=small(),
        name="project",
    )(after_expert, qkv_grad, *pieces)
    column = pl.BlockSpec((rows, span), lambda n: (0, n))
    total = pl.pallas_call(
        join_kernel,
        out_shape=jax.ShapeDtypeStruct((rows, width), BF16),
        grid=(outer,),
        in_specs=[
            pl.BlockSpec((items, rows), lambda n: (0, 0)),
            pl.BlockSpec((items, span), lambda n: (0, n)),
            column,
        ],
        out_specs=column,
        compiler_params=params(8),
        cost_estimate=small(),
        name="join",
    )(picks, returned, token_grad)
    return total[None]


def solution(mesh):
    rows = P("grp", "ctx", None)
    expert = P(("grp", "ctx"), None, None)
    lists = P("grp", "ctx", None, None)
    return jax.shard_map(
        local,
        mesh=mesh,
        in_specs=(rows,) * 5 + (P("ctx", None),) + (expert,) * 3 + (lists, rows, lists),
        out_specs=rows,
        check_vma=False,
    )
```

```python
import functools
import math

import jax
import jax.numpy as jnp
from jax import lax
from jax.experimental import pallas as pl
from jax.experimental.pallas import tpu as pltpu
from jax.sharding import PartitionSpec as P

DH = 128
MIB = 1024 * 1024
FOLD = 8
LARGE = 52
F32 = jnp.float32
BF16 = jnp.bfloat16
LAST = (((1,), (1,)), ((), ()))
FIRST = (((0,), (0,)), ((), ()))
PLAIN = (((1,), (0,)), ((), ()))


def dot(left, right, contract):
    return lax.dot_general(left, right, contract, preferred_element_type=F32)


def in_vmem():
    return pl.BlockSpec(memory_space=pltpu.VMEM)


def in_smem():
    return pl.BlockSpec(memory_space=pltpu.SMEM)


def anywhere():
    return pl.BlockSpec(memory_space=pl.ANY)


def params(mib=6):
    return pltpu.CompilerParams(vmem_limit_bytes=mib * MIB)


def small():
    return pl.CostEstimate(flops=1, bytes_accessed=1, transcendentals=0)


def lane_slice(start, size):
    return pl.ds(pl.multiple_of(start, DH), size)


class Plan:
    def __init__(self):
        self.grp = lax.axis_size("grp")
        self.ctx = lax.axis_size("ctx")
        self.cores = 2 if self.grp % 2 == 0 else 1
        self.cross = self.grp // self.cores
        inner = 1
        while inner * inner * 4 <= self.ctx and self.ctx % (inner * 2) == 0:
            inner *= 2
        self.inner = inner
        self.outer = self.ctx // inner

    def outer_turn(self, k):
        a, b = self.outer, self.inner
        return [(z * b + y, ((z + k) % a) * b + y) for z in range(a) for y in range(b)]

    def inner_turn(self, k):
        a, b = self.outer, self.inner
        return [(z * b + y, z * b + (y + k) % b) for z in range(a) for y in range(b)]

    def pairs(self, go):
        found = []
        for g in range(self.grp):
            x, c = divmod(g, self.cores)
            for at in range(self.ctx):
                z, y = divmod(at, self.inner)
                goal = go(x, c, z, y)
                if goal is not None:
                    x2, c2, z2, y2 = goal
                    to = (x2 % self.cross * self.cores + c2) * self.ctx
                    found.append((g * self.ctx + at, to + z2 * self.inner + y2 % self.inner))
        return found

    def move(self, array, go):
        return lax.ppermute(array, ("grp", "ctx"), self.pairs(go))

    def swap(self, array):
        return self.move(array, lambda x, c, z, y: (x, 1 - c, z, y))


def state_kernel(inner, turn, pos_ref, *refs):
    arrays, out_ref, (q_ref, k_ref, v_ref, g_ref, sems) = refs[:4], refs[4], refs[5:]
    each = out_ref.shape[1]
    lanes = lane_slice(lax.rem(pos_ref[3] + turn, inner) * each, each)
    q_hbm, k_hbm, v_hbm, g_hbm = (array.at[:, lanes] for array in arrays)
    loads = start_loads(
        sems, (v_hbm, v_ref), (k_hbm, k_ref), (g_hbm, g_ref), (q_hbm, q_ref)
    )
    for n, (left, right) in enumerate(((v_ref, k_ref), (g_ref, q_ref))):
        loads[2 * n].wait()
        loads[2 * n + 1].wait()
        for h in range(each // DH):
            head = slice(h * DH, (h + 1) * DH)
            out_ref[n, head, :] = dot(left[:, head], right[:, head], FIRST).astype(BF16)


def total_kernel(inner, outer, pos_ref, *refs):
    ins, outs = refs[:inner], refs[inner:]
    total = ins[0][...].astype(F32)
    for ref in ins[1:]:
        total = total + ref[...].astype(F32)
    values, grads = total[0].astype(BF16), total[1].astype(BF16)
    for k, out in enumerate(outs, 1):
        out[...] = jnp.where(pos_ref[2] + k < outer, values, grads)


def spread_kernel(inner, outer, pos_ref, *refs):
    own, far, outs = refs[:inner], refs[inner : inner + outer - 1], refs[inner + outer - 1 :]
    z, y = pos_ref[2], pos_ref[3]
    shape = own[0].shape[1:]
    before = jnp.zeros(shape, F32)
    after = jnp.zeros(shape, F32)
    for k, ref in enumerate(far, 1):
        piece = ref[...].astype(F32)
        before = before + jnp.where(z >= k, piece, 0.0)
        after = after + jnp.where(z < k, piece, 0.0)
    for i, out in enumerate(outs):
        goal = lax.rem(y + i, inner)
        low, high = before, after
        for k, ref in enumerate(own):
            source = lax.rem(y + inner - k, inner)
            low = low + jnp.where(source < goal, ref[0].astype(F32), 0.0)
            high = high + jnp.where(source > goal, ref[1].astype(F32), 0.0)
        out[0] = low.astype(BF16)
        out[1] = high.astype(BF16)


def near_kernel(scaling, first, pos_ref, q_ref, k_ref, v_ref, g_ref, out_ref):
    rows = q_ref.shape[0]
    half = rows // 2
    early, late = slice(0, half), slice(half, rows)
    row = lax.broadcasted_iota(jnp.int32, (half, half), 0)
    column = lax.broadcasted_iota(jnp.int32, (half, half), 1)

    def scores(left, right, keep):
        value = scaling * dot(left, right, LAST)
        if keep is not None:
            value = jnp.where(keep, value, 0.0)
        return value.astype(BF16)

    def past(left, right, values):
        first = scores(left[early], right[early], row >= column)
        cross = scores(left[late], right[early], None)
        second = scores(left[late], right[late], row >= column)
        low = dot(first, values[early], PLAIN)
        high = dot(cross, values[early], PLAIN) + dot(second, values[late], PLAIN)
        return low, high

    def future(left, right, values):
        first = scores(left[early], right[early], row <= column)
        cross = scores(left[early], right[late], None)
        second = scores(left[late], right[late], row <= column)
        low = dot(first, values[early], PLAIN) + dot(cross, values[late], PLAIN)
        high = dot(second, values[late], PLAIN)
        return low, high

    def one_head(h, carry):
        lanes = lane_slice((first + h) * DH, DH)
        q, k, v, g = q_ref[:, lanes], k_ref[:, lanes], v_ref[:, lanes], g_ref[:, lanes]
        goal = lane_slice(h * DH, DH)
        for n, (low, high) in enumerate((past(g, v, k), future(v, g, q), future(k, q, g))):
            out_ref[n, early, goal] = low.astype(BF16)
            out_ref[n, late, goal] = high.astype(BF16)
        return carry

    lax.fori_loop(0, out_ref.shape[2] // DH, one_head, 0)


def input_rows_kernel(chosen_ref, pad_ref, combine_ref, x_ref, out_ref, picks_ref, *scratch):
    ones, tail, folded = scratch
    rows, width = x_ref.shape
    slots = chosen_ref.shape[3]
    row = lax.broadcasted_iota(jnp.int32, (1, rows), 1)
    lane = lax.broadcasted_iota(jnp.int32, (1, DH), 1)

    def one_slot(n, carry):
        expert, slot = lax.div(n, slots), lax.rem(n, slots)
        live = slot < slots - pad_ref[0, 0, expert]
        token = jnp.where(live, chosen_ref[0, 0, expert, slot], -1)
        ones[pl.ds(n, 1), :] = jnp.where(row == token, 1.0, 0.0)
        weight = jnp.full((1, DH), jnp.where(live, combine_ref[0, 0, expert, slot], 0.0), F32)
        upper = weight.astype(BF16).astype(F32)
        both = jnp.where(lane == 0, upper, jnp.where(lane == 1, weight - upper, 0.0))
        tail[pl.ds(n, 1), :] = both
        return carry

    lax.fori_loop(0, ones.shape[0], one_slot, 0)
    picks = ones[...].astype(BF16)
    picks_ref[...] = picks
    picked = dot(picks, x_ref[...], PLAIN)
    each = folded.shape[0]
    for m in range(each * FOLD):
        part = jnp.zeros_like(tail) if m * DH > width else tail[...]
        if m * DH < width:
            part = picked[:, m * DH : (m + 1) * DH]
        folded[m % each, pl.ds(m // each, ones.shape[0], stride=FOLD), :] = part
    for at in range(each):
        out_ref[:, at * DH : (at + 1) * DH] = folded[at].astype(BF16)


def far_kernel(plan, cuts, scaling, pos_ref, picks_ref, k_ref, v_ref, g_ref, *refs):
    inner = plan.inner
    states, near = refs[:inner], refs[inner : inner + cuts]
    qkv_ref, rows_ref, folded = refs[-3:]
    picks = picks_ref[...]
    x = lax.div(pos_ref[0], plan.cores)
    depth = qkv_ref.shape[1] // plan.cross
    rows, channels = k_ref.shape
    heads = channels // DH
    each = heads // inner
    for h in range(heads):
        lanes = slice(h * DH, (h + 1) * DH)
        turn = lax.rem(pos_ref[3] + inner - h // each, inner)
        inside = slice((h % each) * DH, (h % each + 1) * DH)
        pair = states[0][:, inside, :]
        for i in range(1, inner):
            pair = jnp.where(turn == i, states[i][:, inside, :], pair)
        parts = (
            dot(g_ref[:, lanes], pair[0], PLAIN),
            dot(v_ref[:, lanes], pair[1], PLAIN),
            dot(k_ref[:, lanes], pair[1], LAST),
        )
        share = heads // cuts
        near_lanes = slice((h % share) * DH, (h % share + 1) * DH)
        for n, part in enumerate(parts):
            whole = near[h // share][n, :, near_lanes].astype(F32) + scaling * part
            whole = whole.astype(BF16)
            part_at, inside_at = divmod((n * heads + h) * DH, depth)
            start = lax.rem(x + plan.cross - part_at, plan.cross) * depth + inside_at
            qkv_ref[:, lane_slice(start, DH)] = whole
            start = (n * heads + h) * DH
            fold, at = divmod(start // DH, folded.shape[0])
            folded[at, pl.ds(fold, picks.shape[0], stride=FOLD), :] = dot(picks, whole, PLAIN)
    for at in range(folded.shape[0]):
        rows_ref[:, at * DH : (at + 1) * DH] = folded[at].astype(BF16)


def turn_kernel(pos_ref, in_ref, out_ref):
    out_ref[...] = in_ref[...].T


def turned(plan, weight, pos, mode):
    block = (weight.shape[0], weight.shape[1] // plan.grp)
    cross, cores = plan.cross, plan.cores
    steps = {"own": 1, "part": cores, "whole": plan.grp}[mode]

    def source(n, at):
        if mode == "whole":
            return (0, n)
        return (0, at[0] // cores * cores + n if mode == "part" else at[0])

    def place(n, at):
        if mode != "whole":
            return (n, 0)
        return (lax.rem(at[0] // cores + cross - n // cores, cross) * cores + n % cores, 0)

    return pl.pallas_call(
        turn_kernel,
        out_shape=jax.ShapeDtypeStruct((steps * block[1], weight.shape[0]), BF16),
        grid_spec=pltpu.PrefetchScalarGridSpec(
            num_scalar_prefetch=1,
            grid=(steps,),
            in_specs=[pl.BlockSpec(block, source)],
            out_specs=pl.BlockSpec((block[1], block[0]), place),
        ),
        compiler_params=params(),
        cost_estimate=small(),
        name="turned",
    )(pos, weight)


class Pieces:
    def __init__(self, plan, entries, pos_ref, refs, ring, sems):
        self.plan, self.pos_ref, self.ring, self.sems = plan, pos_ref, ring, sems
        self.core = lax.rem(pos_ref[0], plan.cores)
        self.found = {}
        sources = list(refs)
        for turn, dx, dy, skip, first in entries:
            pair = [sources.pop(0) for _ in range(1 if first is None else 2)]
            self.found.setdefault((turn, dy), []).append((dx, skip, first, pair))
        for n in range(len(self.found)):
            self.copy(n, True)

    def copy(self, n, start):
        depth = self.ring.shape[1] // self.plan.cross
        parts = list(self.found.values())[n]
        for m, (dx, skip, first, pair) in enumerate(parts):
            deep = pair[0].shape[0]
            at = 0 if dx is None else dx * depth + skip * (depth // 2)
            goal = self.ring.at[n, pl.ds(at, deep), :]
            copy = pltpu.make_async_copy(pair[0], goal, self.sems.at[n, m])
            if not start:
                copy.wait()
            elif first is None:
                copy.start()
            else:
                other = pltpu.make_async_copy(pair[1], goal, self.sems.at[n, m])
                pl.when(self.core == first)(copy.start)
                pl.when(self.core != first)(other.start)

    def blocks(self):
        plan = self.plan
        wide = self.ring.shape[2]
        for n, (turn, dy) in enumerate(self.found):
            self.copy(n, False)
            z = lax.rem(self.pos_ref[2] + plan.outer - turn, plan.outer)
            y = lax.rem(self.pos_ref[3] + plan.inner - dy, plan.inner)
            yield lane_slice((z * plan.inner + y) * wide, wide), self.ring.at[n]


def ring_scratch(found):
    wide = found[0][1][0].shape[1]
    depths = {}
    for (turn, _, dy, _, _), buffers in found:
        depths[turn, dy] = depths.get((turn, dy), 0) + buffers[0].shape[0]
    ring = pltpu.VMEM((len(depths), max(depths.values()), wide), BF16)
    return [ring, pltpu.SemaphoreType.DMA((len(depths), len(found)))]


def reach_blocks(plan, pos_ref, rows_ref, pieces, turned_ref, folded):
    x = lax.div(pos_ref[0], plan.cores)
    depth = turned_ref.shape[1] // plan.cross
    count, each = turned_ref.shape[0], folded.shape[0]
    for at in range(each):
        folded[at] = rows_ref[:, at * DH : (at + 1) * DH].astype(F32)
        for fold in range(FOLD):
            part, inside = divmod((fold * each + at) * DH, depth)
            lanes = lane_slice(lax.rem(x + plan.cross - part, plan.cross) * depth + inside, DH)
            rows = folded[at, pl.ds(fold, count, stride=FOLD), :]
            turned_ref[:, lanes] = rows.astype(BF16)
    return [
        (lanes, dot(turned_ref[...], block[...], PLAIN).astype(BF16))
        for lanes, block in pieces.blocks()
    ]


def start_loads(sems, *pairs):
    loads = [pltpu.make_async_copy(x, y, sems.at[n]) for n, (x, y) in enumerate(pairs)]
    for load in loads:
        load.start()
    return loads


def reach_kernel(plan, entries, pos_ref, rows_ref, down_hbm, *refs):
    pieces, (back_ref, turned_ref, folded, down_ref, loaded, ring, sems) = refs[:-7], refs[-7:]
    pieces = Pieces(plan, entries, pos_ref, pieces, ring, sems)
    (load,) = start_loads(loaded, (down_hbm, down_ref))
    blocks = reach_blocks(plan, pos_ref, rows_ref, pieces, turned_ref, folded)
    load.wait()
    back_ref[...] = jnp.zeros_like(back_ref)
    for lanes, grads in blocks:
        back_ref[...] += dot(down_ref[:, lanes], grads, LAST)


def expert_kernel(plan, entries, pos_ref, rows_ref, packed_ref, back_ref, *refs):
    hbm, refs = refs[:3], refs[3:]
    pieces, (out_ref, held, turned_ref, folded, result) = refs[:-13], refs[-13:-8]
    packed, folded_packed = refs[-8:-6]
    (gate_ref, up_ref, down_ref), (loaded, ring, sems) = refs[-6:-3], refs[-3:]
    pieces = Pieces(plan, entries, pos_ref, pieces, ring, sems)
    loads = start_loads(loaded, *zip(hbm, (gate_ref, up_ref, down_ref), strict=True))
    blocks = reach_blocks(plan, pos_ref, rows_ref, pieces, turned_ref, folded)
    width = gate_ref.shape[0]
    each = folded_packed.shape[0]
    for at in range(each):
        folded_packed[at] = packed_ref[:, at * DH : (at + 1) * DH].astype(F32)
        for fold in range(FOLD):
            start = (fold * each + at) * DH
            if start <= width:
                part = folded_packed[at, pl.ds(fold, packed.shape[0], stride=FOLD), :]
                packed[:, start : start + DH] = part.astype(BF16)
    loads[0].wait()
    gate = dot(packed[:, :width], gate_ref[...], PLAIN)
    loads[1].wait()
    up = dot(packed[:, :width], up_ref[...], PLAIN)
    sigma = jax.nn.sigmoid(gate)
    active = gate * sigma
    slope = up * (sigma * (1.0 + gate * (1.0 - sigma)))
    loads[2].wait()
    held[...] = back_ref[...]
    for lanes, grads in blocks:
        held[...] += dot(down_ref[:, lanes], grads, LAST)
    weight = packed[:, width : width + 1].astype(F32)
    weight = weight + packed[:, width + 1 : width + 2].astype(F32)
    hidden = weight * held[...].T
    up_grad = (hidden * active).astype(BF16)
    gate_grad = (hidden * slope).astype(BF16)
    steps = 4
    for n in range(steps):
        some = slice(n * width // steps, (n + 1) * width // steps)
        total = dot(gate_ref[some], gate_grad, LAST) + dot(up_ref[some], up_grad, LAST)
        total = total.T
        for m in range(width // steps // DH):
            fold, at = divmod(n * (width // steps // DH) + m, result.shape[0])
            goal = pl.ds(fold, total.shape[0], stride=FOLD)
            result[at, goal, :] = total[:, m * DH : (m + 1) * DH]
    for at in range(result.shape[0]):
        out_ref[:, at * DH : (at + 1) * DH] = result[at].astype(BF16)


def project_kernel(plan, entries, pos_ref, qkv_hbm, *refs):
    pieces, (out_ref, qkv_ref, loaded, ring, sems) = refs[:-5], refs[-5:]
    (load,) = start_loads(loaded, (qkv_hbm, qkv_ref))
    pieces = Pieces(plan, entries, pos_ref, pieces, ring, sems)
    load.wait()
    half = out_ref.shape[0] // 2
    depth = qkv_ref.shape[1] // plan.cross
    for lanes, block in pieces.blocks():
        for n in range(2):
            rows = slice(n * half, (n + 1) * half)
            total = None
            for dx in range(plan.cross):
                deep = slice(dx * depth, (dx + 1) * depth)
                term = dot(qkv_ref[rows, deep], block[deep, :], PLAIN)
                total = term if total is None else total + term
            out_ref[rows, lanes] = total.astype(BF16)


def join_kernel(picks_ref, returned_ref, token_ref, out_ref, folded, unfolded):
    count, each = picks_ref.shape[0], folded.shape[0]

    @pl.when(pl.program_id(0) == 0)
    def _():
        for at in range(each):
            folded[at] = returned_ref[:, at * DH : (at + 1) * DH].astype(F32)
            for fold in range(FOLD):
                start = (fold * each + at) * DH
                part = folded[at, pl.ds(fold, count, stride=FOLD), :]
                unfolded[:, start : start + DH] = part.astype(BF16)

    size = out_ref.shape[1]
    lanes = lane_slice(pl.program_id(0) * size, size)
    added = dot(picks_ref[...], unfolded[:, lanes], FIRST)
    out_ref[...] = (token_ref[...].astype(F32) + added).astype(BF16)


def together(*values):
    return lax.optimization_barrier(values)


class Turn:
    def __init__(self, plan, turn, held):
        self.plan, self.turn, self.held = plan, turn, held
        self.core = lax.rem(lax.axis_index("grp"), plan.cores)
        self.first = self.mixed(held)

    def mixed(self, array):
        plan, moved = self.plan, {}
        for k in range(1, max(plan.cross, plan.inner)):

            def go(x, c, z, y, k=k):
                if c == 0:
                    return (x + k, c, z, y) if k < plan.cross else None
                return (x, c, z, y + k) if k < plan.inner else None

            moved[k] = plan.move(array, go)
        return moved

    def swap(self):
        self.other = self.plan.swap(self.held)

    def again(self):
        self.second = self.mixed(self.other)

    def turn_corners(self):
        plan = self.plan
        self.corners = {}
        for dx in range(1, plan.cross):
            for dy in range(1, plan.inner):
                sent = self.second[dx]
                if dx != dy:
                    sent = jnp.where(self.core == 0, sent, self.second[dy])

                def go(x, c, z, y, dx=dx, dy=dy):
                    return (x, c, z, y + dy) if c == 0 else (x + dx, c, z, y)

                self.corners[dx, dy] = plan.move(sent, go)

    def pieces(self):
        plan, turn = self.plan, self.turn
        found = [((turn, 0, 0, n, n), (self.held, self.other)) for n in range(2)]
        for k, array in self.first.items():
            first = (array, plan.swap(array))
            second = (self.second[k], plan.swap(self.second[k]))
            if k < plan.cross:
                found.append(((turn, k, 0, 0, 0), first))
                found.append(((turn, k, 0, 1, 0), second))
            if k < plan.inner:
                found.append(((turn, 0, k, 0, 1), second))
                found.append(((turn, 0, k, 1, 1), first))
        for (dx, dy), array in self.corners.items():
            pair = (array, plan.swap(array))
            found.append(((turn, dx, dy, 0, 1), pair))
            found.append(((turn, dx, dy, 1, 0), pair))
        return found


def local(
    inputs,
    queries,
    key_heads,
    value_heads,
    out_grad,
    qkv_weight,
    gate_weight,
    up_weight,
    down_weight,
    chosen,
    pad_counts,
    combine,
):
    plan = Plan()
    rows, width = inputs.shape[1:]
    channels = queries.shape[2]
    heads = channels // DH
    scaling = 1.0 / math.sqrt(plan.ctx * rows * DH)
    q, k, v, g = queries[0], key_heads[0], value_heads[0], out_grad[0]
    gate_mat, up_mat, down_mat = gate_weight[0], up_weight[0], down_weight[0]
    hidden = gate_mat.shape[1]
    experts, slots = chosen.shape[2:]
    items = experts * slots
    inner, outer = plan.inner, plan.outer
    grp_at, ctx_at = lax.axis_index("grp"), lax.axis_index("ctx")
    pos = jnp.stack([grp_at, ctx_at, ctx_at // inner, ctx_at % inner]).astype(jnp.int32)
    across = range(1, plan.cross)
    part = jax.ShapeDtypeStruct((2, channels // inner, DH), BF16)
    own = [None] * inner
    for i in reversed(range(inner)):
        own[i] = pl.pallas_call(
            functools.partial(state_kernel, inner, i),
            out_shape=part,
            in_specs=[in_smem()] + [anywhere()] * 4,
            out_specs=in_vmem(),
            scratch_shapes=[pltpu.VMEM((rows, channels // inner), BF16)] * 4
            + [pltpu.SemaphoreType.DMA((4,))],
            compiler_params=params(LARGE),
            cost_estimate=small(),
            name="states",
        )(pos, q, k, v, g)
    shares = [lax.ppermute(own[i], "ctx", plan.inner_turn(i)) for i in range(1, inner)]
    (later, *_) = together(pos, own[-1])
    held = turned(plan, qkv_weight, later, "own")
    held = lax.ppermute(held, "ctx", plan.outer_turn(1))
    packed_each = pl.cdiv(width + DH, FOLD * DH)
    packed, picks = pl.pallas_call(
        input_rows_kernel,
        out_shape=[
            jax.ShapeDtypeStruct((items * FOLD, packed_each * DH), BF16),
            jax.ShapeDtypeStruct((items, rows), BF16),
        ],
        in_specs=[in_smem()] * 3 + [in_vmem()],
        out_specs=[in_vmem()] * 2,
        scratch_shapes=[
            *(pltpu.VMEM((items, rows), F32), pltpu.VMEM((items, DH), F32)),
            pltpu.VMEM((packed_each, items * FOLD, DH), F32),
        ],
        compiler_params=params(),
        cost_estimate=small(),
        name="input_rows",
    )(chosen, pad_counts, combine, inputs[0])
    packed, picks, *shares = together(packed, picks, own[0], *shares)
    totals = pl.pallas_call(
        functools.partial(total_kernel, inner, outer),
        out_shape=[jax.ShapeDtypeStruct(part.shape[1:], BF16)] * (outer - 1),
        in_specs=[in_smem()] + [in_vmem()] * inner,
        out_specs=[in_vmem()] * (outer - 1),
        compiler_params=params(),
        cost_estimate=small(),
        name="totals",
    )(pos, *shares)
    after_totals, *totals = together(pos, *totals)
    far = [lax.ppermute(totals[i - 1], "ctx", plan.outer_turn(i)) for i in range(1, outer)]
    aside = turned(plan, qkv_weight, after_totals, "part")
    beside = [
        plan.move(aside, lambda x, c, z, y, dy=dy: (x, c, z, y + dy) if c == 1 else None)
        for dy in range(1, inner)
    ]

    cuts = 2 if heads % 2 == 0 else 1

    def near_part(cut, after):
        return pl.pallas_call(
            functools.partial(near_kernel, scaling, cut * (heads // cuts)),
            out_shape=jax.ShapeDtypeStruct((3, rows, channels // cuts), BF16),
            in_specs=[in_smem()] + [in_vmem()] * 4,
            out_specs=in_vmem(),
            compiler_params=params(),
            cost_estimate=small(),
            name="near",
        )(after, q, k, v, g)

    near = [near_part(0, after_totals)]
    after_near, held, near[0], *arrived = together(after_totals, held, near[0], *far[:1])
    far[:1] = arrived
    turns = []
    if outer > 1:
        turns.append(Turn(plan, 1, held))
        turns[0].swap()
    if outer > 2:
        held = lax.ppermute(held, "ctx", plan.outer_turn(1))
    near += [near_part(cut, after_near) for cut in range(1, cuts)]
    if turns:
        near[-1], turns[0].other = together(near[-1], turns[0].other)
        turns[0].again()

    def exchange(array):
        return lax.all_to_all(array, ("grp", "ctx"), split_axis=0, concat_axis=0, tiled=True)

    whole = turned(plan, qkv_weight, after_near, "whole")
    shares[0], whole, *arrived = together(shares[0], whole, *far, *near, *beside)
    far, near = arrived[: outer - 1], arrived[outer - 1 : outer - 1 + cuts]
    beside = arrived[outer - 1 + cuts :]
    sums = pl.pallas_call(
        functools.partial(spread_kernel, inner, outer),
        out_shape=[part] * inner,
        in_specs=[in_smem()] + [in_vmem()] * (inner + outer - 1),
        out_specs=[in_vmem()] * inner,
        compiler_params=params(),
        cost_estimate=small(),
        name="sums",
    )(pos, *shares, *far)
    states = [lax.ppermute(sums[i], "ctx", plan.inner_turn(i)) for i in range(1, inner)]
    state = sums[0]
    behind = []
    if turns:
        state, held, *arrived = together(state, held, *turns[0].first.values())
        turns[0].first = dict(zip(turns[0].first, arrived, strict=True))
    moving = dict(turns[0].second) if turns else {}
    if outer > 2:
        turns.append(Turn(plan, 2, held))
        turns[1].swap()
        if outer > 3:
            held = lax.ppermute(held, "ctx", plan.outer_turn(1))
        behind = [held, turns[1].other, *turns[1].first.values()]
    state, *arrived = together(state, *states, *moving.values(), *behind)
    states, arrived = [state, *arrived[: len(states)]], arrived[len(states) :]
    if turns:
        turns[0].second = dict(zip(moving, arrived, strict=False))
        turns[0].turn_corners()
        arrived = arrived[len(moving) :]
    if outer > 2:
        held, turns[1].other, *arrived = arrived
        turns[1].first = dict(zip(turns[1].first, arrived, strict=True))
        turns[1].again()

    folded_rows = pltpu.VMEM((3 * channels // FOLD // DH, items * FOLD, DH), F32)
    folded_result = pltpu.VMEM((width // FOLD // DH, items * FOLD, DH), F32)
    qkv_grad, sent_rows = pl.pallas_call(
        functools.partial(far_kernel, plan, cuts, scaling),
        out_shape=[
            jax.ShapeDtypeStruct((rows, 3 * channels), BF16),
            jax.ShapeDtypeStruct((items * FOLD, 3 * channels // FOLD), BF16),
        ],
        in_specs=[in_smem()] + [in_vmem()] * (4 + inner + cuts),
        out_specs=[in_vmem()] * 2,
        scratch_shapes=[folded_rows],
        compiler_params=params(8),
        cost_estimate=small(),
        name="far",
    )(pos, picks, k, v, g, *states, *near)
    for turn in range(3, outer):
        if turn > 3:
            held = lax.ppermute(held, "ctx", plan.outer_turn(1))
        turns.append(Turn(plan, turn, held))
        turns[-1].swap()
    qkv_grad, *beside = together(qkv_grad, *beside)
    aside = [
        [plan.move(x0, lambda x, c, z, y, dx=dx: (x + dx, c, z, y) if c == 1 else None) for dx in across]
        for x0 in beside
    ]
    others = [turn.other for turn in turns[2:]]
    for turn in turns[2:]:
        turn.again()
    sent_rows, *_ = together(sent_rows, *others)
    grad_rows = exchange(sent_rows)
    waits = [turn.first for turn in turns] + [turns[0].corners] + [turn.second for turn in turns[:2]]
    waits.append(dict(enumerate(beside)))
    waits += [dict(enumerate(arrays)) for arrays in aside]
    flat = [array for wait in waits for array in wait.values()]
    grad_rows, packed, *arrived = together(grad_rows, packed, *flat)
    came = exchange(packed)
    for wait in waits:
        for key in wait:
            wait[key] = arrived.pop(0)
    beside, aside = waits[-1 - len(aside)], waits[len(waits) - len(aside) :]
    if outer > 2:
        turns[1].turn_corners()
    found = [((0, None, 0, 0, None), (whole,))]
    for turn in turns[:-1]:
        found.extend(turn.pieces())
    for dy in range(1, inner):
        for dx in range(plan.cross):
            array = beside[dy - 1] if dx == 0 else aside[dy - 1][dx - 1]
            copied = plan.move(array, lambda x, c, z, y: (x, 0, z, y) if c == 1 else None)
            found.append(((0, dx, dy, 0, 1), (array, copied)))

    def some(keep):
        kept = [item for item in found if keep(item[0][0])]
        return kept, [item[0] for item in kept], [x for item in kept for x in item[1]]

    span = inner * qkv_weight.shape[0]

    turned_rows = pltpu.VMEM((items, 3 * channels), BF16)
    qkv_held = pltpu.VMEM((rows, 3 * channels), BF16)
    down_held = pltpu.VMEM((hidden, width), BF16)

    split = max(outer - 2, 1)
    kept, entries, pieces = some(lambda turn: turn < split)
    back = pl.pallas_call(
        functools.partial(reach_kernel, plan, entries),
        out_shape=jax.ShapeDtypeStruct((hidden, items), F32),
        in_specs=[in_smem(), in_vmem()] + [anywhere()] * (1 + len(pieces)),
        out_specs=in_vmem(),
        scratch_shapes=[
            *(turned_rows, folded_rows, down_held, pltpu.SemaphoreType.DMA((1,))),
            *ring_scratch(kept),
        ],
        compiler_params=params(LARGE),
        cost_estimate=small(),
        name="reach",
    )(pos, grad_rows, down_mat, *pieces)
    if turns:
        last = turns[-1]
        if outer > 2:
            last.turn_corners()
        back, *arrived = together(back, *last.corners.values())
        last.corners = dict(zip(last.corners, arrived, strict=True))
    if turns:
        found.extend(turns[-1].pieces())
    kept, entries, pieces = some(lambda turn: turn >= split)
    slot_grad = pl.pallas_call(
        functools.partial(expert_kernel, plan, entries),
        out_shape=jax.ShapeDtypeStruct((items * FOLD, width // FOLD), BF16),
        in_specs=[in_smem()] + [in_vmem()] * 3 + [anywhere()] * (3 + len(pieces)),
        out_specs=in_vmem(),
        scratch_shapes=[
            *(pltpu.VMEM((hidden, items), F32), turned_rows, folded_rows, folded_result),
            *(pltpu.VMEM((items, width + DH), BF16),),
            pltpu.VMEM((packed_each, items * FOLD, DH), F32),
            *[pltpu.VMEM((width, hidden), BF16)] * 2,
            *(down_held, pltpu.SemaphoreType.DMA((3,))),
            *ring_scratch(kept),
        ],
        compiler_params=params(LARGE),
        cost_estimate=small(),
        name="expert",
    )(pos, grad_rows, came, back, gate_mat, up_mat, down_mat, *pieces)
    returned = exchange(slot_grad)
    kept, entries, pieces = some(lambda turn: True)
    (after_expert, *_) = together(pos, slot_grad)
    token_grad = pl.pallas_call(
        functools.partial(project_kernel, plan, entries),
        out_shape=jax.ShapeDtypeStruct((rows, width), BF16),
        in_specs=[in_smem()] + [anywhere()] * (1 + len(pieces)),
        out_specs=in_vmem(),
        scratch_shapes=[qkv_held, pltpu.SemaphoreType.DMA((1,)), *ring_scratch(kept)],
        compiler_params=params(LARGE),
        cost_estimate=small(),
        name="project",
    )(after_expert, qkv_grad, *pieces)
    column = pl.BlockSpec((rows, span), lambda n: (0, n))
    total = pl.pallas_call(
        join_kernel,
        out_shape=jax.ShapeDtypeStruct((rows, width), BF16),
        grid=(outer,),
        in_specs=[
            pl.BlockSpec((items, rows), lambda n: (0, 0)),
            pl.BlockSpec((items * FOLD, width // FOLD), lambda n: (0, 0)),
            column,
        ],
        out_specs=column,
        scratch_shapes=[folded_result, pltpu.VMEM((items, width), BF16)],
        compiler_params=params(8),
        cost_estimate=small(),
        name="join",
    )(picks, returned, token_grad)
    return total[None]


def solution(mesh):
    rows = P("grp", "ctx", None)
    expert = P(("grp", "ctx"), None, None)
    lists = P("grp", "ctx", None, None)
    return jax.shard_map(
        local,
        mesh=mesh,
        in_specs=(rows,) * 5 + (P("ctx", None),) + (expert,) * 3 + (lists, rows, lists),
        out_specs=rows,
        check_vma=False,
    )
```

```python
import functools
import math

import jax
import jax.numpy as jnp
from jax import lax
from jax.experimental import pallas as pl
from jax.experimental.pallas import tpu as pltpu
from jax.sharding import PartitionSpec as P

DH = 128
MIB = 1024 * 1024
FOLD = 8
LARGE = 52
F32 = jnp.float32
BF16 = jnp.bfloat16
LAST = (((1,), (1,)), ((), ()))
FIRST = (((0,), (0,)), ((), ()))
PLAIN = (((1,), (0,)), ((), ()))


def dot(left, right, contract):
    return lax.dot_general(left, right, contract, preferred_element_type=F32)


def in_vmem():
    return pl.BlockSpec(memory_space=pltpu.VMEM)


def in_smem():
    return pl.BlockSpec(memory_space=pltpu.SMEM)


def anywhere():
    return pl.BlockSpec(memory_space=pl.ANY)


def params(mib=6):
    return pltpu.CompilerParams(vmem_limit_bytes=mib * MIB)


def small():
    return pl.CostEstimate(flops=1, bytes_accessed=1, transcendentals=0)


def lane_slice(start, size):
    return pl.ds(pl.multiple_of(start, DH), size)


class Plan:
    def __init__(self):
        self.grp = lax.axis_size("grp")
        self.ctx = lax.axis_size("ctx")
        self.cores = 2 if self.grp % 2 == 0 else 1
        self.cross = self.grp // self.cores
        inner = 1
        while inner * inner * 4 <= self.ctx and self.ctx % (inner * 2) == 0:
            inner *= 2
        self.inner = inner
        self.outer = self.ctx // inner

    def outer_turn(self, k):
        a, b = self.outer, self.inner
        return [(z * b + y, ((z + k) % a) * b + y) for z in range(a) for y in range(b)]

    def inner_turn(self, k):
        a, b = self.outer, self.inner
        return [(z * b + y, z * b + (y + k) % b) for z in range(a) for y in range(b)]

    def pairs(self, go):
        found = []
        for g in range(self.grp):
            x, c = divmod(g, self.cores)
            for at in range(self.ctx):
                z, y = divmod(at, self.inner)
                goal = go(x, c, z, y)
                if goal is not None:
                    x2, c2, z2, y2 = goal
                    to = (x2 % self.cross * self.cores + c2) * self.ctx
                    found.append((g * self.ctx + at, to + z2 * self.inner + y2 % self.inner))
        return found

    def move(self, array, go):
        return lax.ppermute(array, ("grp", "ctx"), self.pairs(go))

    def swap(self, array):
        return self.move(array, lambda x, c, z, y: (x, 1 - c, z, y))


def state_kernel(inner, turn, pos_ref, *refs):
    arrays, out_ref, (q_ref, k_ref, v_ref, g_ref, sems) = refs[:4], refs[4], refs[5:]
    each = out_ref.shape[1]
    lanes = lane_slice(lax.rem(pos_ref[3] + turn, inner) * each, each)
    q_hbm, k_hbm, v_hbm, g_hbm = (array.at[:, lanes] for array in arrays)
    loads = start_loads(
        sems, (v_hbm, v_ref), (k_hbm, k_ref), (g_hbm, g_ref), (q_hbm, q_ref)
    )
    for n, (left, right) in enumerate(((v_ref, k_ref), (g_ref, q_ref))):
        loads[2 * n].wait()
        loads[2 * n + 1].wait()
        for h in range(each // DH):
            head = slice(h * DH, (h + 1) * DH)
            out_ref[n, head, :] = dot(left[:, head], right[:, head], FIRST).astype(BF16)


def total_kernel(inner, outer, pos_ref, *refs):
    ins, outs = refs[:inner], refs[inner:]
    total = ins[0][...].astype(F32)
    for ref in ins[1:]:
        total = total + ref[...].astype(F32)
    values, grads = total[0].astype(BF16), total[1].astype(BF16)
    for k, out in enumerate(outs, 1):
        out[...] = jnp.where(pos_ref[2] + k < outer, values, grads)


def spread_kernel(inner, outer, pos_ref, *refs):
    own, far, outs = refs[:inner], refs[inner : inner + outer - 1], refs[inner + outer - 1 :]
    z, y = pos_ref[2], pos_ref[3]
    shape = own[0].shape[1:]
    before = jnp.zeros(shape, F32)
    after = jnp.zeros(shape, F32)
    for k, ref in enumerate(far, 1):
        piece = ref[...].astype(F32)
        before = before + jnp.where(z >= k, piece, 0.0)
        after = after + jnp.where(z < k, piece, 0.0)
    for i, out in enumerate(outs):
        goal = lax.rem(y + i, inner)
        low, high = before, after
        for k, ref in enumerate(own):
            source = lax.rem(y + inner - k, inner)
            low = low + jnp.where(source < goal, ref[0].astype(F32), 0.0)
            high = high + jnp.where(source > goal, ref[1].astype(F32), 0.0)
        out[0] = low.astype(BF16)
        out[1] = high.astype(BF16)


def near_kernel(scaling, first, pos_ref, q_ref, k_ref, v_ref, g_ref, out_ref):
    rows = q_ref.shape[0]
    half = rows // 2
    early, late = slice(0, half), slice(half, rows)
    row = lax.broadcasted_iota(jnp.int32, (half, half), 0)
    column = lax.broadcasted_iota(jnp.int32, (half, half), 1)

    def scores(left, right, keep):
        value = scaling * dot(left, right, LAST)
        if keep is not None:
            value = jnp.where(keep, value, 0.0)
        return value.astype(BF16)

    def past(left, right, values):
        first = scores(left[early], right[early], row >= column)
        cross = scores(left[late], right[early], None)
        second = scores(left[late], right[late], row >= column)
        low = dot(first, values[early], PLAIN)
        high = dot(cross, values[early], PLAIN) + dot(second, values[late], PLAIN)
        return low, high

    def future(left, right, values):
        first = scores(left[early], right[early], row <= column)
        cross = scores(left[early], right[late], None)
        second = scores(left[late], right[late], row <= column)
        low = dot(first, values[early], PLAIN) + dot(cross, values[late], PLAIN)
        high = dot(second, values[late], PLAIN)
        return low, high

    def one_head(h, carry):
        lanes = lane_slice((first + h) * DH, DH)
        q, k, v, g = q_ref[:, lanes], k_ref[:, lanes], v_ref[:, lanes], g_ref[:, lanes]
        goal = lane_slice(h * DH, DH)
        for n, (low, high) in enumerate((past(g, v, k), future(v, g, q), future(k, q, g))):
            out_ref[n, early, goal] = low.astype(BF16)
            out_ref[n, late, goal] = high.astype(BF16)
        return carry

    lax.fori_loop(0, out_ref.shape[2] // DH, one_head, 0)


def input_rows_kernel(chosen_ref, pad_ref, combine_ref, x_ref, out_ref, picks_ref, *scratch):
    ones, tail, folded = scratch
    rows, width = x_ref.shape
    slots = chosen_ref.shape[3]
    row = lax.broadcasted_iota(jnp.int32, (1, rows), 1)
    lane = lax.broadcasted_iota(jnp.int32, (1, DH), 1)

    def one_slot(n, carry):
        expert, slot = lax.div(n, slots), lax.rem(n, slots)
        live = slot < slots - pad_ref[0, 0, expert]
        token = jnp.where(live, chosen_ref[0, 0, expert, slot], -1)
        ones[pl.ds(n, 1), :] = jnp.where(row == token, 1.0, 0.0)
        weight = jnp.full((1, DH), jnp.where(live, combine_ref[0, 0, expert, slot], 0.0), F32)
        upper = weight.astype(BF16).astype(F32)
        both = jnp.where(lane == 0, upper, jnp.where(lane == 1, weight - upper, 0.0))
        tail[pl.ds(n, 1), :] = both
        return carry

    lax.fori_loop(0, ones.shape[0], one_slot, 0)
    picks = ones[...].astype(BF16)
    picks_ref[...] = picks
    picked = dot(picks, x_ref[...], PLAIN)
    each = folded.shape[0]
    for m in range(each * FOLD):
        part = jnp.zeros_like(tail) if m * DH > width else tail[...]
        if m * DH < width:
            part = picked[:, m * DH : (m + 1) * DH]
        folded[m % each, pl.ds(m // each, ones.shape[0], stride=FOLD), :] = part
    for at in range(each):
        out_ref[:, at * DH : (at + 1) * DH] = folded[at].astype(BF16)


def far_kernel(plan, cuts, scaling, pos_ref, picks_ref, k_ref, v_ref, g_ref, *refs):
    inner = plan.inner
    states, near = refs[:inner], refs[inner : inner + cuts]
    qkv_ref, rows_ref, folded = refs[-3:]
    picks = picks_ref[...]
    x = lax.div(pos_ref[0], plan.cores)
    depth = qkv_ref.shape[1] // plan.cross
    rows, channels = k_ref.shape
    heads = channels // DH
    each = heads // inner
    for h in range(heads):
        lanes = slice(h * DH, (h + 1) * DH)
        turn = lax.rem(pos_ref[3] + inner - h // each, inner)
        inside = slice((h % each) * DH, (h % each + 1) * DH)
        pair = states[0][:, inside, :]
        for i in range(1, inner):
            pair = jnp.where(turn == i, states[i][:, inside, :], pair)
        parts = (
            dot(g_ref[:, lanes], pair[0], PLAIN),
            dot(v_ref[:, lanes], pair[1], PLAIN),
            dot(k_ref[:, lanes], pair[1], LAST),
        )
        share = heads // cuts
        near_lanes = slice((h % share) * DH, (h % share + 1) * DH)
        for n, part in enumerate(parts):
            whole = near[h // share][n, :, near_lanes].astype(F32) + scaling * part
            whole = whole.astype(BF16)
            part_at, inside_at = divmod((n * heads + h) * DH, depth)
            start = lax.rem(x + plan.cross - part_at, plan.cross) * depth + inside_at
            qkv_ref[:, lane_slice(start, DH)] = whole
            start = (n * heads + h) * DH
            fold, at = divmod(start // DH, folded.shape[0])
            folded[at, pl.ds(fold, picks.shape[0], stride=FOLD), :] = dot(picks, whole, PLAIN)
    for at in range(folded.shape[0]):
        rows_ref[:, at * DH : (at + 1) * DH] = folded[at].astype(BF16)


def turn_kernel(pos_ref, in_ref, out_ref):
    out_ref[...] = in_ref[...].T


def turned(plan, weight, pos, mode):
    block = (weight.shape[0], weight.shape[1] // plan.grp)
    cross, cores = plan.cross, plan.cores
    steps = {"own": 1, "part": cores, "whole": plan.grp}[mode]

    def source(n, at):
        if mode == "whole":
            return (0, n)
        return (0, at[0] // cores * cores + n if mode == "part" else at[0])

    def place(n, at):
        if mode != "whole":
            return (n, 0)
        return (lax.rem(at[0] // cores + cross - n // cores, cross) * cores + n % cores, 0)

    return pl.pallas_call(
        turn_kernel,
        out_shape=jax.ShapeDtypeStruct((steps * block[1], weight.shape[0]), BF16),
        grid_spec=pltpu.PrefetchScalarGridSpec(
            num_scalar_prefetch=1,
            grid=(steps,),
            in_specs=[pl.BlockSpec(block, source)],
            out_specs=pl.BlockSpec((block[1], block[0]), place),
        ),
        compiler_params=params(),
        cost_estimate=small(),
        name="turned",
    )(pos, weight)


class Pieces:
    def __init__(self, plan, entries, pos_ref, refs, ring, sems):
        self.plan, self.pos_ref, self.ring, self.sems = plan, pos_ref, ring, sems
        self.core = lax.rem(pos_ref[0], plan.cores)
        self.found = {}
        sources = list(refs)
        for turn, dx, dy, skip, first in entries:
            pair = [sources.pop(0) for _ in range(1 if first is None else 2)]
            self.found.setdefault((turn, dy), []).append((dx, skip, first, pair))
        for n in range(len(self.found)):
            self.copy(n, True)

    def copy(self, n, start):
        depth = self.ring.shape[1] // self.plan.cross
        parts = list(self.found.values())[n]
        for m, (dx, skip, first, pair) in enumerate(parts):
            deep = pair[0].shape[0]
            at = 0 if dx is None else dx * depth + skip * (depth // 2)
            goal = self.ring.at[n, pl.ds(at, deep), :]
            copy = pltpu.make_async_copy(pair[0], goal, self.sems.at[n, m])
            if not start:
                copy.wait()
            elif first is None:
                copy.start()
            else:
                other = pltpu.make_async_copy(pair[1], goal, self.sems.at[n, m])
                pl.when(self.core == first)(copy.start)
                pl.when(self.core != first)(other.start)

    def blocks(self):
        plan = self.plan
        wide = self.ring.shape[2]
        for n, (turn, dy) in enumerate(self.found):
            self.copy(n, False)
            z = lax.rem(self.pos_ref[2] + plan.outer - turn, plan.outer)
            y = lax.rem(self.pos_ref[3] + plan.inner - dy, plan.inner)
            yield lane_slice((z * plan.inner + y) * wide, wide), self.ring.at[n]


def ring_scratch(found):
    wide = found[0][1][0].shape[1]
    depths = {}
    for (turn, _, dy, _, _), buffers in found:
        depths[turn, dy] = depths.get((turn, dy), 0) + buffers[0].shape[0]
    ring = pltpu.VMEM((len(depths), max(depths.values()), wide), BF16)
    return [ring, pltpu.SemaphoreType.DMA((len(depths), len(found)))]


def reach_blocks(plan, pos_ref, rows_ref, pieces, turned_ref, folded):
    x = lax.div(pos_ref[0], plan.cores)
    depth = turned_ref.shape[1] // plan.cross
    count, each = turned_ref.shape[0], folded.shape[0]
    for at in range(each):
        folded[at] = rows_ref[:, at * DH : (at + 1) * DH].astype(F32)
        for fold in range(FOLD):
            part, inside = divmod((fold * each + at) * DH, depth)
            lanes = lane_slice(lax.rem(x + plan.cross - part, plan.cross) * depth + inside, DH)
            rows = folded[at, pl.ds(fold, count, stride=FOLD), :]
            turned_ref[:, lanes] = rows.astype(BF16)
    return [
        (lanes, dot(turned_ref[...], block[...], PLAIN).astype(BF16))
        for lanes, block in pieces.blocks()
    ]


def start_loads(sems, *pairs):
    loads = [pltpu.make_async_copy(x, y, sems.at[n]) for n, (x, y) in enumerate(pairs)]
    for load in loads:
        load.start()
    return loads


def reach_kernel(plan, entries, pos_ref, rows_ref, down_hbm, *refs):
    pieces, (back_ref, turned_ref, folded, down_ref, loaded, ring, sems) = refs[:-7], refs[-7:]
    pieces = Pieces(plan, entries, pos_ref, pieces, ring, sems)
    (load,) = start_loads(loaded, (down_hbm, down_ref))
    blocks = reach_blocks(plan, pos_ref, rows_ref, pieces, turned_ref, folded)
    load.wait()
    back_ref[...] = jnp.zeros_like(back_ref)
    for lanes, grads in blocks:
        back_ref[...] += dot(down_ref[:, lanes], grads, LAST)


def expert_kernel(plan, entries, pos_ref, rows_ref, packed_ref, back_ref, *refs):
    hbm, refs = refs[:3], refs[3:]
    pieces, (out_ref, held, turned_ref, folded, result) = refs[:-13], refs[-13:-8]
    packed, folded_packed = refs[-8:-6]
    (gate_ref, up_ref, down_ref), (loaded, ring, sems) = refs[-6:-3], refs[-3:]
    pieces = Pieces(plan, entries, pos_ref, pieces, ring, sems)
    loads = start_loads(loaded, *zip(hbm, (gate_ref, up_ref, down_ref), strict=True))
    blocks = reach_blocks(plan, pos_ref, rows_ref, pieces, turned_ref, folded)
    width = gate_ref.shape[0]
    each = folded_packed.shape[0]
    for at in range(each):
        folded_packed[at] = packed_ref[:, at * DH : (at + 1) * DH].astype(F32)
        for fold in range(FOLD):
            start = (fold * each + at) * DH
            if start <= width:
                part = folded_packed[at, pl.ds(fold, packed.shape[0], stride=FOLD), :]
                packed[:, start : start + DH] = part.astype(BF16)
    loads[0].wait()
    gate = dot(packed[:, :width], gate_ref[...], PLAIN)
    loads[1].wait()
    up = dot(packed[:, :width], up_ref[...], PLAIN)
    sigma = jax.nn.sigmoid(gate)
    active = gate * sigma
    slope = up * (sigma * (1.0 + gate * (1.0 - sigma)))
    loads[2].wait()
    held[...] = back_ref[...]
    for lanes, grads in blocks:
        held[...] += dot(down_ref[:, lanes], grads, LAST)
    weight = packed[:, width : width + 1].astype(F32)
    weight = weight + packed[:, width + 1 : width + 2].astype(F32)
    hidden = weight * held[...].T
    up_grad = (hidden * active).astype(BF16)
    gate_grad = (hidden * slope).astype(BF16)
    steps = 4
    for n in range(steps):
        some = slice(n * width // steps, (n + 1) * width // steps)
        total = dot(gate_ref[some], gate_grad, LAST) + dot(up_ref[some], up_grad, LAST)
        total = total.T
        for m in range(width // steps // DH):
            fold, at = divmod(n * (width // steps // DH) + m, result.shape[0])
            goal = pl.ds(fold, total.shape[0], stride=FOLD)
            result[at, goal, :] = total[:, m * DH : (m + 1) * DH]
    for at in range(result.shape[0]):
        out_ref[:, at * DH : (at + 1) * DH] = result[at].astype(BF16)


def project_kernel(plan, entries, pos_ref, qkv_hbm, *refs):
    pieces, (out_ref, qkv_ref, loaded, ring, sems) = refs[:-5], refs[-5:]
    (load,) = start_loads(loaded, (qkv_hbm, qkv_ref))
    pieces = Pieces(plan, entries, pos_ref, pieces, ring, sems)
    load.wait()
    half = out_ref.shape[0] // 2
    depth = qkv_ref.shape[1] // plan.cross
    for lanes, block in pieces.blocks():
        for n in range(2):
            rows = slice(n * half, (n + 1) * half)
            total = None
            for dx in range(plan.cross):
                deep = slice(dx * depth, (dx + 1) * depth)
                term = dot(qkv_ref[rows, deep], block[deep, :], PLAIN)
                total = term if total is None else total + term
            out_ref[rows, lanes] = total.astype(BF16)


def join_kernel(picks_ref, returned_ref, token_ref, out_ref, folded, unfolded):
    count, each = picks_ref.shape[0], folded.shape[0]

    @pl.when(pl.program_id(0) == 0)
    def _():
        for at in range(each):
            folded[at] = returned_ref[:, at * DH : (at + 1) * DH].astype(F32)
            for fold in range(FOLD):
                start = (fold * each + at) * DH
                part = folded[at, pl.ds(fold, count, stride=FOLD), :]
                unfolded[:, start : start + DH] = part.astype(BF16)

    size = out_ref.shape[1]
    lanes = lane_slice(pl.program_id(0) * size, size)
    added = dot(picks_ref[...], unfolded[:, lanes], FIRST)
    out_ref[...] = (token_ref[...].astype(F32) + added).astype(BF16)


def together(*values):
    return lax.optimization_barrier(values)


class Turn:
    def __init__(self, plan, turn, held):
        self.plan, self.turn, self.held = plan, turn, held
        self.core = lax.rem(lax.axis_index("grp"), plan.cores)
        self.first = self.mixed(held)

    def mixed(self, array):
        plan, moved = self.plan, {}
        for k in range(1, max(plan.cross, plan.inner)):

            def go(x, c, z, y, k=k):
                if c == 0:
                    return (x + k, c, z, y) if k < plan.cross else None
                return (x, c, z, y + k) if k < plan.inner else None

            moved[k] = plan.move(array, go)
        return moved

    def swap(self):
        self.other = self.plan.swap(self.held)

    def again(self):
        self.second = self.mixed(self.other)

    def turn_corners(self):
        plan = self.plan
        self.corners = {}
        for dx in range(1, plan.cross):
            for dy in range(1, plan.inner):
                sent = self.second[dx]
                if dx != dy:
                    sent = jnp.where(self.core == 0, sent, self.second[dy])

                def go(x, c, z, y, dx=dx, dy=dy):
                    return (x, c, z, y + dy) if c == 0 else (x + dx, c, z, y)

                self.corners[dx, dy] = plan.move(sent, go)

    def pieces(self):
        plan, turn = self.plan, self.turn
        found = [((turn, 0, 0, n, n), (self.held, self.other)) for n in range(2)]
        for k, array in self.first.items():
            first = (array, plan.swap(array))
            second = (self.second[k], plan.swap(self.second[k]))
            if k < plan.cross:
                found.append(((turn, k, 0, 0, 0), first))
                found.append(((turn, k, 0, 1, 0), second))
            if k < plan.inner:
                found.append(((turn, 0, k, 0, 1), second))
                found.append(((turn, 0, k, 1, 1), first))
        for (dx, dy), array in self.corners.items():
            pair = (array, plan.swap(array))
            found.append(((turn, dx, dy, 0, 1), pair))
            found.append(((turn, dx, dy, 1, 0), pair))
        return found


def local(
    inputs,
    queries,
    key_heads,
    value_heads,
    out_grad,
    qkv_weight,
    gate_weight,
    up_weight,
    down_weight,
    chosen,
    pad_counts,
    combine,
):
    plan = Plan()
    rows, width = inputs.shape[1:]
    channels = queries.shape[2]
    heads = channels // DH
    scaling = 1.0 / math.sqrt(plan.ctx * rows * DH)
    q, k, v, g = queries[0], key_heads[0], value_heads[0], out_grad[0]
    gate_mat, up_mat, down_mat = gate_weight[0], up_weight[0], down_weight[0]
    hidden = gate_mat.shape[1]
    experts, slots = chosen.shape[2:]
    items = experts * slots
    inner, outer = plan.inner, plan.outer
    grp_at, ctx_at = lax.axis_index("grp"), lax.axis_index("ctx")
    pos = jnp.stack([grp_at, ctx_at, ctx_at // inner, ctx_at % inner]).astype(jnp.int32)
    across = range(1, plan.cross)
    part = jax.ShapeDtypeStruct((2, channels // inner, DH), BF16)
    own = [None] * inner
    for i in reversed(range(inner)):
        own[i] = pl.pallas_call(
            functools.partial(state_kernel, inner, i),
            out_shape=part,
            in_specs=[in_smem()] + [anywhere()] * 4,
            out_specs=in_vmem(),
            scratch_shapes=[pltpu.VMEM((rows, channels // inner), BF16)] * 4
            + [pltpu.SemaphoreType.DMA((4,))],
            compiler_params=params(LARGE),
            cost_estimate=small(),
            name="states",
        )(pos, q, k, v, g)
    shares = [lax.ppermute(own[i], "ctx", plan.inner_turn(i)) for i in range(1, inner)]
    (later, *_) = together(pos, own[-1])
    held = turned(plan, qkv_weight, later, "own")
    held = lax.ppermute(held, "ctx", plan.outer_turn(1))
    packed_each = pl.cdiv(width + DH, FOLD * DH)
    packed, picks = pl.pallas_call(
        input_rows_kernel,
        out_shape=[
            jax.ShapeDtypeStruct((items * FOLD, packed_each * DH), BF16),
            jax.ShapeDtypeStruct((items, rows), BF16),
        ],
        in_specs=[in_smem()] * 3 + [in_vmem()],
        out_specs=[in_vmem()] * 2,
        scratch_shapes=[
            *(pltpu.VMEM((items, rows), F32), pltpu.VMEM((items, DH), F32)),
            pltpu.VMEM((packed_each, items * FOLD, DH), F32),
        ],
        compiler_params=params(),
        cost_estimate=small(),
        name="input_rows",
    )(chosen, pad_counts, combine, inputs[0])
    packed, picks, *shares = together(packed, picks, own[0], *shares)
    totals = pl.pallas_call(
        functools.partial(total_kernel, inner, outer),
        out_shape=[jax.ShapeDtypeStruct(part.shape[1:], BF16)] * (outer - 1),
        in_specs=[in_smem()] + [in_vmem()] * inner,
        out_specs=[in_vmem()] * (outer - 1),
        compiler_params=params(),
        cost_estimate=small(),
        name="totals",
    )(pos, *shares)
    after_totals, *totals = together(pos, *totals)
    far = [lax.ppermute(totals[i - 1], "ctx", plan.outer_turn(i)) for i in range(1, outer)]
    aside = turned(plan, qkv_weight, after_totals, "part")
    beside = [
        plan.move(aside, lambda x, c, z, y, dy=dy: (x, c, z, y + dy) if c == 1 else None)
        for dy in range(1, inner)
    ]

    cuts = 2 if heads % 2 == 0 else 1

    def near_part(cut, after):
        return pl.pallas_call(
            functools.partial(near_kernel, scaling, cut * (heads // cuts)),
            out_shape=jax.ShapeDtypeStruct((3, rows, channels // cuts), BF16),
            in_specs=[in_smem()] + [in_vmem()] * 4,
            out_specs=in_vmem(),
            compiler_params=params(),
            cost_estimate=small(),
            name="near",
        )(after, q, k, v, g)

    near = [near_part(0, after_totals)]
    after_near, held, near[0], *arrived = together(after_totals, held, near[0], *far[:1])
    far[:1] = arrived
    turns = []
    if outer > 1:
        turns.append(Turn(plan, 1, held))
        turns[0].swap()
    if outer > 2:
        held = lax.ppermute(held, "ctx", plan.outer_turn(1))
    near += [near_part(cut, after_near) for cut in range(1, cuts)]
    if turns:
        near[-1], turns[0].other = together(near[-1], turns[0].other)
        turns[0].again()

    def exchange(array):
        return lax.all_to_all(array, ("grp", "ctx"), split_axis=0, concat_axis=0, tiled=True)

    whole = turned(plan, qkv_weight, after_near, "whole")
    shares[0], whole, *arrived = together(shares[0], whole, *far, *near, *beside)
    far, near = arrived[: outer - 1], arrived[outer - 1 : outer - 1 + cuts]
    beside = arrived[outer - 1 + cuts :]
    sums = pl.pallas_call(
        functools.partial(spread_kernel, inner, outer),
        out_shape=[part] * inner,
        in_specs=[in_smem()] + [in_vmem()] * (inner + outer - 1),
        out_specs=[in_vmem()] * inner,
        compiler_params=params(),
        cost_estimate=small(),
        name="sums",
    )(pos, *shares, *far)
    states = [lax.ppermute(sums[i], "ctx", plan.inner_turn(i)) for i in range(1, inner)]
    state = sums[0]
    behind = []
    if turns:
        state, held, *arrived = together(state, held, *turns[0].first.values())
        turns[0].first = dict(zip(turns[0].first, arrived, strict=True))
    moving = dict(turns[0].second) if turns else {}
    if outer > 2:
        turns.append(Turn(plan, 2, held))
        turns[1].swap()
        if outer > 3:
            held = lax.ppermute(held, "ctx", plan.outer_turn(1))
        behind = [held, turns[1].other, *turns[1].first.values()]
    state, *arrived = together(state, *states, *moving.values(), *behind)
    states, arrived = [state, *arrived[: len(states)]], arrived[len(states) :]
    if turns:
        turns[0].second = dict(zip(moving, arrived, strict=False))
        turns[0].turn_corners()
        arrived = arrived[len(moving) :]
    if outer > 2:
        held, turns[1].other, *arrived = arrived
        turns[1].first = dict(zip(turns[1].first, arrived, strict=True))
        turns[1].again()

    folded_rows = pltpu.VMEM((3 * channels // FOLD // DH, items * FOLD, DH), F32)
    folded_result = pltpu.VMEM((width // FOLD // DH, items * FOLD, DH), F32)
    qkv_grad, sent_rows = pl.pallas_call(
        functools.partial(far_kernel, plan, cuts, scaling),
        out_shape=[
            jax.ShapeDtypeStruct((rows, 3 * channels), BF16),
            jax.ShapeDtypeStruct((items * FOLD, 3 * channels // FOLD), BF16),
        ],
        in_specs=[in_smem()] + [in_vmem()] * (4 + inner + cuts),
        out_specs=[in_vmem()] * 2,
        scratch_shapes=[folded_rows],
        compiler_params=params(8),
        cost_estimate=small(),
        name="far",
    )(pos, picks, k, v, g, *states, *near)
    for turn in range(3, outer):
        if turn > 3:
            held = lax.ppermute(held, "ctx", plan.outer_turn(1))
        turns.append(Turn(plan, turn, held))
        turns[-1].swap()
    qkv_grad, *beside = together(qkv_grad, *beside)
    aside = [
        [plan.move(x0, lambda x, c, z, y, dx=dx: (x + dx, c, z, y) if c == 1 else None) for dx in across]
        for x0 in beside
    ]
    others = [turn.other for turn in turns[2:]]
    for turn in turns[2:]:
        turn.again()
    sent_rows, *_ = together(sent_rows, *others)
    grad_rows = exchange(sent_rows)
    waits = [turn.first for turn in turns[:2]] + [turns[0].corners] + [turn.second for turn in turns[:2]]
    waits.append(dict(enumerate(beside)))
    waits += [dict(enumerate(arrays)) for arrays in aside]
    flat = [array for wait in waits for array in wait.values()]
    grad_rows, packed, *arrived = together(grad_rows, packed, *flat)
    came = exchange(packed)
    for wait in waits:
        for key in wait:
            wait[key] = arrived.pop(0)
    beside, aside = waits[-1 - len(aside)], waits[len(waits) - len(aside) :]
    if outer > 2:
        turns[1].turn_corners()
    found = [((0, None, 0, 0, None), (whole,))]
    for turn in turns[:-1]:
        found.extend(turn.pieces())
    for dy in range(1, inner):
        for dx in range(plan.cross):
            array = beside[dy - 1] if dx == 0 else aside[dy - 1][dx - 1]
            copied = plan.move(array, lambda x, c, z, y: (x, 0, z, y) if c == 1 else None)
            found.append(((0, dx, dy, 0, 1), (array, copied)))

    def some(keep):
        kept = [item for item in found if keep(item[0][0])]
        return kept, [item[0] for item in kept], [x for item in kept for x in item[1]]

    span = inner * qkv_weight.shape[0]

    turned_rows = pltpu.VMEM((items, 3 * channels), BF16)
    qkv_held = pltpu.VMEM((rows, 3 * channels), BF16)
    down_held = pltpu.VMEM((hidden, width), BF16)

    split = max(outer - 2, 1)
    kept, entries, pieces = some(lambda turn: turn < split)
    back = pl.pallas_call(
        functools.partial(reach_kernel, plan, entries),
        out_shape=jax.ShapeDtypeStruct((hidden, items), F32),
        in_specs=[in_smem(), in_vmem()] + [anywhere()] * (1 + len(pieces)),
        out_specs=in_vmem(),
        scratch_shapes=[
            *(turned_rows, folded_rows, down_held, pltpu.SemaphoreType.DMA((1,))),
            *ring_scratch(kept),
        ],
        compiler_params=params(LARGE),
        cost_estimate=small(),
        name="reach",
    )(pos, grad_rows, down_mat, *pieces)
    if turns:
        last = turns[-1]
        if outer > 2:
            last.turn_corners()
        back, *arrived = together(back, *last.corners.values())
        last.corners = dict(zip(last.corners, arrived, strict=True))
    if turns:
        found.extend(turns[-1].pieces())
    kept, entries, pieces = some(lambda turn: turn >= split)
    slot_grad = pl.pallas_call(
        functools.partial(expert_kernel, plan, entries),
        out_shape=jax.ShapeDtypeStruct((items * FOLD, width // FOLD), BF16),
        in_specs=[in_smem()] + [in_vmem()] * 3 + [anywhere()] * (3 + len(pieces)),
        out_specs=in_vmem(),
        scratch_shapes=[
            *(pltpu.VMEM((hidden, items), F32), turned_rows, folded_rows, folded_result),
            *(pltpu.VMEM((items, width + DH), BF16),),
            pltpu.VMEM((packed_each, items * FOLD, DH), F32),
            *[pltpu.VMEM((width, hidden), BF16)] * 2,
            *(down_held, pltpu.SemaphoreType.DMA((3,))),
            *ring_scratch(kept),
        ],
        compiler_params=params(LARGE),
        cost_estimate=small(),
        name="expert",
    )(pos, grad_rows, came, back, gate_mat, up_mat, down_mat, *pieces)
    returned = exchange(slot_grad)
    kept, entries, pieces = some(lambda turn: True)
    (after_expert, *_) = together(pos, slot_grad)
    token_grad = pl.pallas_call(
        functools.partial(project_kernel, plan, entries),
        out_shape=jax.ShapeDtypeStruct((rows, width), BF16),
        in_specs=[in_smem()] + [anywhere()] * (1 + len(pieces)),
        out_specs=in_vmem(),
        scratch_shapes=[qkv_held, pltpu.SemaphoreType.DMA((1,)), *ring_scratch(kept)],
        compiler_params=params(LARGE),
        cost_estimate=small(),
        name="project",
    )(after_expert, qkv_grad, *pieces)
    column = pl.BlockSpec((rows, span), lambda n: (0, n))
    total = pl.pallas_call(
        join_kernel,
        out_shape=jax.ShapeDtypeStruct((rows, width), BF16),
        grid=(outer,),
        in_specs=[
            pl.BlockSpec((items, rows), lambda n: (0, 0)),
            pl.BlockSpec((items * FOLD, width // FOLD), lambda n: (0, 0)),
            column,
        ],
        out_specs=column,
        scratch_shapes=[folded_result, pltpu.VMEM((items, width), BF16)],
        compiler_params=params(8),
        cost_estimate=small(),
        name="join",
    )(picks, returned, token_grad)
    return total[None]


def solution(mesh):
    rows = P("grp", "ctx", None)
    expert = P(("grp", "ctx"), None, None)
    lists = P("grp", "ctx", None, None)
    return jax.shard_map(
        local,
        mesh=mesh,
        in_specs=(rows,) * 5 + (P("ctx", None),) + (expert,) * 3 + (lists, rows, lists),
        out_specs=rows,
        check_vma=False,
    )
```
